32 devices in a mesh: frame: 4 (over y, x), space: 8 (over z, core).
Axes of the slice: x: 2, y: 2, z: 4, core: 2. Of those that a mesh axis runs over, the one named last changes fastest.
Arguments:
- qkv_now: bfloat16 [1024, 16, 384], P('space', 'frame'), as said below
- past_cache: bfloat16 [4, 1024, 16, 256], P('frame', 'space'), may hold values from -6 to 6
- frame_rank: int32 [4], replicated, may hold values from 0 to 3, each once
- frame_depth: int32 [8], replicated, may hold values from 0 to 4, as said below
- tile_lists: int32 [8, 8], replicated, may hold values from 0 to 1, as said below
Outputs:
- attended: bfloat16 [1024, 2048], P('space', 'frame')
The draws below stay inside these ranges and needn't reach their ends.
Inputs may be any that keep to these rules, and one draw needn't show every extreme that they name: Entries of qkv_now lie within -5 to 5. `frame_depth`: some tile sees every past frame. `tile_lists`: entry [t, u] is 1 exactly where the distance between tiles t and u around the closed loop of 8 tiles is at most a radius of tile t; the diagonal is 1 and some tile sees all tiles.
All inputs are finite; a program needn't handle non-finite values.
Results may differ from the reference program's by a relative error of at most 0.01.
Values may be sent and summed in bfloat16 or wider, within the bound.
A program may use at most 64 MiB of HBM per device.

```python
import math
import jax
import jax.numpy as jnp
from jax import lax

HEADS = 16
HEAD_DIM = 128
TOK_DEV = 128
TILES = 8
CUR_TOK = 1024
PAST = 4


def draw_qkv_now(key, part):
    key = jax.random.fold_in(key, 11)
    first = jax.random.fold_in(key, 0)
    shape = (CUR_TOK, HEADS, 3 * HEAD_DIM)
    values = jax.random.truncated_normal(first, -5.0, 5.0, shape, jnp.float32)
    return values.astype(jnp.bfloat16)


def draw_frame_depth(key, part):
    key = jax.random.fold_in(key, 13)
    first, second = jax.random.split(key)
    depth = jax.random.randint(first, (TILES,), 0, PAST + 1, dtype=jnp.int32)
    chosen = jax.random.randint(second, (), 0, TILES, dtype=jnp.int32)
    return jnp.where(jnp.arange(TILES, dtype=jnp.int32) == chosen, PAST, depth).astype(jnp.int32)


def draw_tile_lists(key, part):
    key = jax.random.fold_in(key, 12)
    first, second = jax.random.split(key)
    radius = jax.random.randint(first, (TILES,), 0, TILES // 2 + 1, dtype=jnp.int32)
    chosen = jax.random.randint(second, (), 0, TILES, dtype=jnp.int32)
    indices = jnp.arange(TILES, dtype=jnp.int32)
    radius = jnp.where(indices == chosen, TILES // 2, radius)
    apart = jnp.abs(indices[:, None] - indices[None, :])
    beside_all = jnp.minimum(apart, TILES - apart)
    return (beside_all <= radius[:, None]).astype(jnp.int32)


def steps_of(key, shape, cuts, low, top_value):
    factor_of = 1.0
    for axis_at, shards_of in cuts:
        steps = jax.random.uniform(jax.random.fold_in(jax.random.fold_in(key, 6), axis_at), (shards_of,), jnp.float32, low / len(cuts), top_value / len(cuts))
        factor_of = factor_of * jnp.repeat(jnp.exp(steps), shape[axis_at] // shards_of).reshape((-1,) + (1,) * (len(shape) - 1 - axis_at))
    return factor_of


def normal_values(own_key, shape, deviation, limit, shards=(), kind=jnp.bfloat16):
    level = steps_of(own_key, shape, shards, -0.22, 0.18) if shards else 1.0
    values = jax.random.normal(own_key, shape, jnp.float32) * deviation * level
    return jnp.minimum(jnp.maximum(values, -limit), limit).astype(kind)


def setup_inputs(seed: int = 0) -> dict:
    seeds = jax.random.split(jax.random.key(seed), 6)
    qkv_now = draw_qkv_now(jax.random.fold_in(seeds[5], 71), 0)
    past_cache = normal_values(seeds[1], (PAST, CUR_TOK, HEADS, 2 * HEAD_DIM), 1.0, 6.0, ((0, 4), (1, 8)))
    frame_rank = jax.random.permutation(seeds[2], PAST).astype(jnp.int32)
    frame_depth = draw_frame_depth(jax.random.fold_in(seeds[5], 71), 0)
    tile_lists = draw_tile_lists(jax.random.fold_in(seeds[5], 71), 0)
    return {"qkv_now": qkv_now, "past_cache": past_cache, "frame_rank": frame_rank, "frame_depth": frame_depth, "tile_lists": tile_lists}


NEG = -1e+30

def reference(qkv_now, past_cache, frame_rank, frame_depth, tile_lists):
    score_scale = 1.0 / math.sqrt(HEAD_DIM)
    group_len = (PAST + 1) * TOK_DEV
    frame_seen = (frame_rank[None, :] >= PAST - frame_depth[:, None]).astype(jnp.float32)

    def one_tile(tile):
        queries = lax.dynamic_slice_in_dim(qkv_now, (tile * TOK_DEV).astype(jnp.int32), TOK_DEV, 0)
        row_list = lax.dynamic_index_in_dim(tile_lists, tile, 0, False).astype(jnp.float32)
        seen = lax.dynamic_index_in_dim(frame_seen, tile, 0, False)
        group_seen = jnp.concatenate([seen, jnp.ones((1,), jnp.float32)])
        visible = jnp.broadcast_to(row_list[:, None, None] * group_seen[None, :, None], (TILES, PAST + 1, TOK_DEV)).reshape(TILES, group_len)

        def one_head(head):
            query = lax.dynamic_index_in_dim(queries, head, 1, False)[:, :HEAD_DIM].astype(jnp.float32)
            current = lax.dynamic_index_in_dim(qkv_now, head, 1, False)[:, HEAD_DIM:].reshape(TILES, 1, TOK_DEV, 2 * HEAD_DIM)
            cached = lax.dynamic_index_in_dim(past_cache, head, 2, False).reshape(PAST, TILES, TOK_DEV, 2 * HEAD_DIM).transpose(1, 0, 2, 3)
            grouped = jnp.concatenate([cached, current], 1).reshape(TILES, group_len, 2 * HEAD_DIM).astype(jnp.float32)
            scores = jnp.einsum('qd,ugd->qug', query, grouped[..., :HEAD_DIM], precision=lax.Precision.HIGHEST) * score_scale
            masked = jnp.where(visible[None] > 0, scores, NEG)
            peak = lax.optimization_barrier(jnp.max(masked, axis=2))
            weights = jnp.exp(masked - peak[..., None]) * visible[None]
            totals = lax.optimization_barrier(jnp.sum(weights, axis=2))
            rounded = weights.astype(jnp.bfloat16).astype(jnp.float32)
            weighted = jnp.einsum('qug,ugd->qud', rounded, grouped[..., HEAD_DIM:], precision=lax.Precision.HIGHEST)
            safe = jnp.maximum(totals, 1.0)
            share = (weighted / safe[..., None]).astype(jnp.bfloat16).astype(jnp.float32)
            lse = peak + jnp.log(safe)
            top = lax.optimization_barrier(jnp.max(lse, axis=1, keepdims=True))
            factor = jnp.exp(lse - top)
            return lax.optimization_barrier(jnp.sum(share * factor[..., None], axis=1)) / lax.optimization_barrier(jnp.sum(factor, axis=1))[:, None]
        return lax.map(one_head, jnp.arange(HEADS, dtype=jnp.int32))
    result = lax.map(one_tile, jnp.arange(TILES, dtype=jnp.int32))
    return result.transpose(0, 2, 1, 3).reshape(CUR_TOK, HEADS * HEAD_DIM).astype(jnp.bfloat16)
```

```python
import functools
import math

import jax
import jax.numpy as jnp
from jax import lax
from jax.experimental import pallas as pl
from jax.experimental.pallas import tpu as pltpu
from jax.sharding import PartitionSpec as P

HIDDEN = -1e30
FLOOR = -1e29
MESH = pl.DeviceIdType.MESH
LOG2E = math.log2(math.e)


def attend(
    frames,
    members,
    heads,
    rank_ref,
    depth_ref,
    lists_ref,
    past_ref,
    qkv_ref,
    out_ref,
    kv,
    queries,
    values,
    share_out,
    share_in,
    lse_out,
    lse_in,
    local_sem,
    past_send,
    past_recv,
    fwd_send,
    fwd_recv,
    query_send,
    query_recv,
    share_send,
    share_recv,
    lse_send,
    lse_recv,
):
    toks = past_ref.shape[1]
    dim = past_ref.shape[2] // 2
    scale = LOG2E / math.sqrt(dim)
    fi = lax.axis_index("frame")
    si = lax.axis_index("space")
    group = si // 2
    core = si % 2
    peer = (fi, group * 2 + 1 - core)

    def frame_at(slot):
        return lax.rem(fi + slot, frames)

    def tile_at(slot):
        return lax.rem(group + slot, members) * 2 + core

    local = [
        [
            pltpu.make_async_copy(past_ref.at[fi * heads + h], kv.at[0, h, 0], local_sem.at[h, 0]),
            pltpu.make_async_copy(
                qkv_ref.at[h, :, pl.ds(dim, 2 * dim)], kv.at[0, h, frames], local_sem.at[h, 1]
            ),
            pltpu.make_async_copy(
                qkv_ref.at[h, :, pl.ds(0, dim)], queries.at[h, 0], local_sem.at[h, 2]
            ),
        ]
        for h in range(heads)
    ]
    for copies in local:
        for copy in copies:
            copy.start()

    def remote(src, dst, send_sem, recv_sem, device):
        return pltpu.make_async_remote_copy(
            src_ref=src,
            dst_ref=dst,
            send_sem=send_sem,
            recv_sem=recv_sem,
            device_id=device,
            device_id_type=MESH,
        )

    past_in = {}
    query_in = {}
    forward = {}
    for h in range(heads):
        for j in range(1, frames):
            to = frame_at(frames - j)
            past_in[h, j] = remote(
                past_ref.at[to * heads + h],
                kv.at[0, h, j],
                past_send.at[h, j],
                past_recv.at[h, j],
                (to, si),
            )
        for j in range(1, members):
            query_in[h, j] = remote(
                qkv_ref.at[h, :, pl.ds(0, dim)],
                queries.at[h, j],
                query_send.at[h, j],
                query_recv.at[h, j],
                (fi, tile_at(members - j)),
            )
        for j in range(frames + 1):
            if j == 0:
                src = past_ref.at[fi * heads + h]
            elif j == frames:
                src = qkv_ref.at[h, :, pl.ds(dim, 2 * dim)]
            else:
                src = kv.at[0, h, j]
            forward[h, j] = remote(
                src, kv.at[1, h, j], fwd_send.at[h, j], fwd_recv.at[h, j], peer
            )

    barrier = pltpu.get_barrier_semaphore()
    partners = [(frame_at(j), si) for j in range(1, frames)]
    partners += [(fi, tile_at(j)) for j in range(1, members)]
    partners.append(peer)
    for partner in partners:
        pl.semaphore_signal(barrier, inc=1, device_id=partner, device_id_type=MESH)
    pl.semaphore_wait(barrier, len(partners))

    for h in range(heads):
        for j in range(1, frames):
            past_in[h, j].start()
        for j in range(1, members):
            query_in[h, j].start()
        forward[h, 0].start()
        forward[h, frames].start()

    lse_out[...] = jnp.zeros_like(lse_out)
    lse_in[0] = jnp.zeros_like(lse_in[0])

    def pass_on(h):
        for j in range(1, frames):
            past_in[h, j].wait_recv()
            forward[h, j].start()

    def bias_of(key_tile, slot, tile):
        sees = lists_ref[tile, key_tile] > 0
        if slot < frames:
            sees = jnp.logical_and(
                sees, rank_ref[frame_at(slot)] >= frames - depth_ref[tile]
            )
        return jnp.where(sees, 0.0, HIDDEN)

    key_tiles = (si, group * 2 + 1 - core)
    span = (frames + 1) * toks
    lanes = lax.broadcasted_iota(jnp.int32, (1, 2 * toks), 1)
    share_copies = {}

    def compute(h, pair):
        slots = (2 * pair, 2 * pair + 1)
        query = queries[h, slots[0] : slots[0] + 2].reshape(2 * toks, dim)
        tiles = [tile_at(j) for j in slots]
        scores = []
        biases = []
        peak = jnp.full((1, 2 * toks), FLOOR, jnp.float32)
        for side in range(2):
            keys = kv[side, h, :, :, :dim].reshape(span, dim)
            score = lax.dot_general(
                keys, query, (((1,), (1,)), ((), ())), preferred_element_type=jnp.float32
            )
            scores.append(score)
            for slot in range(frames + 1):
                bias = jnp.where(
                    lanes < toks,
                    bias_of(key_tiles[side], slot, tiles[0]),
                    bias_of(key_tiles[side], slot, tiles[1]),
                )
                biases.append(bias)
                block = score[slot * toks : (slot + 1) * toks]
                peak = jnp.maximum(peak, jnp.max(block, axis=0, keepdims=True) * scale + bias)
        total = jnp.zeros((1, 2 * toks), jnp.float32)
        weighted = jnp.zeros((dim, 2 * toks), jnp.float32)
        for side in range(2):
            weights = []
            for slot in range(frames + 1):
                block = scores[side][slot * toks : (slot + 1) * toks]
                shift = peak - biases[side * (frames + 1) + slot]
                weight = jnp.exp2(block * scale - shift)
                total += jnp.sum(weight, axis=0, keepdims=True)
                weights.append(weight.astype(jnp.bfloat16))
            weighted += jnp.dot(
                values[h % 2, side],
                jnp.concatenate(weights, 0),
                preferred_element_type=jnp.float32,
            )
        safe = jnp.maximum(total, 1.0)
        share = (weighted * (1.0 / safe)).astype(jnp.bfloat16)
        lse = peak + jnp.log(safe) * LOG2E
        for at, j in enumerate(slots):
            part = share[:, at * toks : (at + 1) * toks]
            lse_part = lse[:, at * toks : (at + 1) * toks]
            if j == 0:
                share_in[h, 0] = part
                lse_in[0, h : h + 1, :] = lse_part
            else:
                share_out[h, j] = part
                lse_out[j, h : h + 1, :] = lse_part
                back = members - j
                copy = remote(
                    share_out.at[h, j],
                    share_in.at[h, back],
                    share_send.at[h, back],
                    share_recv.at[h, back],
                    (fi, tile_at(j)),
                )
                copy.start()
                share_copies[h, back] = copy

    pass_on(0)
    for h in range(heads):
        for copy in local[h]:
            copy.wait()
        for j in range(frames + 1):
            forward[h, j].wait_recv()
        for side in range(2):
            for slot in range(frames + 1):
                values[h % 2, side, :, slot * toks : (slot + 1) * toks] = kv[
                    side, h, slot, :, dim:
                ].T
        for at, pair in enumerate(reversed(range(members // 2))):
            for j in (2 * pair, 2 * pair + 1):
                if j > 0:
                    query_in[h, j].wait_recv()
            compute(h, pair)
            if at == 0 and h + 1 < heads:
                pass_on(h + 1)

    lse_copies = {}
    for j in range(1, members):
        back = members - j
        lse_copies[back] = remote(
            lse_out.at[j], lse_in.at[back], lse_send.at[back], lse_recv.at[back], (fi, tile_at(j))
        )
        lse_copies[back].start()
    for j in range(1, members):
        lse_copies[j].wait_recv()
    for h in range(heads):
        for j in range(1, members):
            share_copies[h, j].wait_recv()
        rows = [lse_in[j, h : h + 1, :] for j in range(members)]
        top = functools.reduce(jnp.maximum, rows)
        factors = [jnp.exp2(row - top) for row in rows]
        denominator = functools.reduce(jnp.add, factors)
        summed = functools.reduce(
            jnp.add,
            [share_in[h, j].astype(jnp.float32) * factors[j] for j in range(members)],
        )
        out_ref[:, h * dim : (h + 1) * dim] = (summed / denominator).T.astype(out_ref.dtype)

    for copies in (past_in, query_in, forward, share_copies, lse_copies):
        for copy in copies.values():
            copy.wait_send()


def body(qkv_now, past_cache, frame_rank, frame_depth, tile_lists):
    toks, heads, width = qkv_now.shape
    dim = width // 3
    frames = lax.axis_size("frame")
    members = lax.axis_size("space") // 2
    past = jnp.transpose(past_cache[0], (1, 0, 2))
    qkv = jnp.transpose(qkv_now, (1, 0, 2))
    lse_rows = -(-heads // 8) * 8
    dma = pltpu.SemaphoreType.DMA
    smem = pl.BlockSpec(memory_space=pltpu.SMEM)
    return pl.pallas_call(
        functools.partial(attend, frames, members, heads),
        out_shape=jax.ShapeDtypeStruct((toks, heads * dim), jnp.bfloat16),
        in_specs=[smem, smem, smem] + [pl.BlockSpec(memory_space=pl.ANY)] * 2,
        out_specs=pl.BlockSpec(memory_space=pltpu.VMEM),
        scratch_shapes=[
            pltpu.VMEM((2, heads, frames + 1, toks, 2 * dim), jnp.bfloat16),
            pltpu.VMEM((heads, members, toks, dim), jnp.bfloat16),
            pltpu.VMEM((2, 2, dim, (frames + 1) * toks), jnp.bfloat16),
            pltpu.VMEM((heads, members, dim, toks), jnp.bfloat16),
            pltpu.VMEM((heads, members, dim, toks), jnp.bfloat16),
            pltpu.VMEM((members, lse_rows, toks), jnp.float32),
            pltpu.VMEM((members, lse_rows, toks), jnp.float32),
            dma((heads, 3)),
            dma((heads, frames)),
            dma((heads, frames)),
            dma((heads, frames + 1)),
            dma((heads, frames + 1)),
            dma((heads, members)),
            dma((heads, members)),
            dma((heads, members)),
            dma((heads, members)),
            dma((members,)),
            dma((members,)),
        ],
        compiler_params=pltpu.CompilerParams(
            collective_id=0, has_side_effects=True, vmem_limit_bytes=48 * 1024 * 1024
        ),
    )(frame_rank, frame_depth, tile_lists, past, qkv)


def solution(mesh):
    in_specs = (P("space", "frame", None), P("frame", "space", None, None), P(), P(), P())
    out_specs = P("space", "frame")
    return jax.shard_map(body, mesh=mesh, in_specs=in_specs, out_specs=out_specs, check_vma=False)
```

```python
import functools
import math

import jax
import jax.numpy as jnp
from jax import lax
from jax.experimental import pallas as pl
from jax.experimental.pallas import tpu as pltpu
from jax.sharding import PartitionSpec as P

HIDDEN = -1e30
FLOOR = -1e29
MESH = pl.DeviceIdType.MESH
LOG2E = math.log2(math.e)


def attend(
    frames,
    members,
    heads,
    rank_ref,
    depth_ref,
    lists_ref,
    past_ref,
    qkv_ref,
    out_ref,
    kv,
    queries,
    values,
    near_out,
    near_in,
    far_out,
    relay_in,
    far_in,
    near_lse_out,
    near_lse_in,
    far_lse_out,
    relay_lse_in,
    far_lse_in,
    held,
    held_lse,
    local_sem,
    past_send,
    past_recv,
    fwd_send,
    fwd_recv,
    query_send,
    query_recv,
    near_sem,
    far_sem,
    relay_recv,
    far_recv,
):
    toks = past_ref.shape[1]
    dim = past_ref.shape[2] // 2
    scale = LOG2E / math.sqrt(dim)
    fi = lax.axis_index("frame")
    si = lax.axis_index("space")
    group = si // 2
    core = si % 2
    peer = (fi, group * 2 + 1 - core)
    size = members // 2
    half = group // size
    place = group - half * size
    other = 1 - half
    inward = 1 - 2 * half
    outermost = jnp.logical_or(group == 0, group == members - 1)
    innermost = jnp.logical_or(group == size - 1, group == size)
    passes = jnp.logical_or(group == 1, group == members - 2)
    end_from = jnp.where(group == 1, members - 1, 0)
    end_to = members - 1 - end_from

    def frame_at(slot):
        return lax.rem(fi + slot, frames)

    def device_of(member):
        return (fi, member * 2 + core)

    def remote(src, dst, send_sem, recv_sem, device):
        return pltpu.make_async_remote_copy(
            src_ref=src,
            dst_ref=dst,
            send_sem=send_sem,
            recv_sem=recv_sem,
            device_id=device,
            device_id_type=MESH,
        )

    local = [
        [
            pltpu.make_async_copy(past_ref.at[fi * heads + h], kv.at[0, h, 0], local_sem.at[h, 0]),
            pltpu.make_async_copy(
                qkv_ref.at[h, :, pl.ds(dim, 2 * dim)], kv.at[0, h, frames], local_sem.at[h, 1]
            ),
            pltpu.make_async_copy(
                qkv_ref.at[h, :, pl.ds(0, dim)], queries.at[h, group], local_sem.at[h, 2]
            ),
        ]
        for h in range(heads)
    ]
    for copies in local:
        for copy in copies:
            copy.start()

    past_in = {}
    forward = {}
    query_out = {}
    query_on = {}
    for h in range(heads):
        for j in range(1, frames):
            to = frame_at(frames - j)
            past_in[h, j] = remote(
                past_ref.at[to * heads + h],
                kv.at[0, h, j],
                past_send.at[h, j],
                past_recv.at[h, j],
                (to, si),
            )
        for j in range(1, members):
            to = lax.rem(group + j, members)
            query_out[h, j] = (
                jnp.abs(to - group) != members - 1,
                remote(
                    qkv_ref.at[h, :, pl.ds(0, dim)],
                    queries.at[h, group],
                    query_send.at[h, j],
                    query_recv.at[h, group],
                    device_of(to),
                ),
            )
        query_on[h] = remote(
            queries.at[h, end_from],
            queries.at[h, end_from],
            query_send.at[h, 0],
            query_recv.at[h, end_from],
            device_of(end_to),
        )
        for j in range(frames + 1):
            if j == 0:
                src = past_ref.at[fi * heads + h]
            elif j == frames:
                src = qkv_ref.at[h, :, pl.ds(dim, 2 * dim)]
            else:
                src = kv.at[0, h, j]
            forward[h, j] = remote(
                src, kv.at[1, h, j], fwd_send.at[h, j], fwd_recv.at[h, j], peer
            )

    def query_wait(h, member):
        remote(
            queries.at[h, member],
            queries.at[h, member],
            query_send.at[h, 0],
            query_recv.at[h, member],
            peer,
        ).wait_recv()

    barrier = pltpu.get_barrier_semaphore()
    partners = [(frame_at(j), si) for j in range(1, frames)]
    partners += [device_of(lax.rem(group + j, members)) for j in range(1, members)]
    partners.append(peer)
    for partner in partners:
        pl.semaphore_signal(barrier, inc=1, device_id=partner, device_id_type=MESH)
    pl.semaphore_wait(barrier, len(partners))

    for h in range(heads):
        for j in range(1, frames):
            past_in[h, j].start()
        for j in range(1, members):
            pl.when(query_out[h, j][0])(query_out[h, j][1].start)
        forward[h, 0].start()
        forward[h, frames].start()

    near_lse_out[...] = jnp.zeros_like(near_lse_out)
    far_lse_out[...] = jnp.zeros_like(far_lse_out)

    def pass_on(h):
        @pl.when(passes)
        def _():
            query_wait(h, end_from)
            query_on[h].start()

        for j in range(1, frames):
            past_in[h, j].wait_recv()
            forward[h, j].start()

    def bias_of(key_tile, slot, tile):
        sees = lists_ref[tile, key_tile] > 0
        if slot < frames:
            sees = jnp.logical_and(
                sees, rank_ref[frame_at(slot)] >= frames - depth_ref[tile]
            )
        return jnp.where(sees, 0.0, HIDDEN)

    key_tiles = (si, group * 2 + 1 - core)
    span = (frames + 1) * toks
    lanes = lax.broadcasted_iota(jnp.int32, (1, 2 * toks), 1)

    def compute(h, first):
        query = queries[h, pl.ds(first, 2)].reshape(2 * toks, dim)
        tiles = [(first + at) * 2 + core for at in range(2)]
        scores = []
        biases = []
        peak = jnp.full((1, 2 * toks), FLOOR, jnp.float32)
        for side in range(2):
            keys = kv[side, h, :, :, :dim].reshape(span, dim)
            score = lax.dot_general(
                keys, query, (((1,), (1,)), ((), ())), preferred_element_type=jnp.float32
            )
            scores.append(score)
            for slot in range(frames + 1):
                bias = jnp.where(
                    lanes < toks,
                    bias_of(key_tiles[side], slot, tiles[0]),
                    bias_of(key_tiles[side], slot, tiles[1]),
                )
                biases.append(bias)
                block = score[slot * toks : (slot + 1) * toks]
                peak = jnp.maximum(peak, jnp.max(block, axis=0, keepdims=True) * scale + bias)
        total = jnp.zeros((1, 2 * toks), jnp.float32)
        weighted = jnp.zeros((dim, 2 * toks), jnp.float32)
        for side in range(2):
            weights = []
            for slot in range(frames + 1):
                block = scores[side][slot * toks : (slot + 1) * toks]
                shift = peak - biases[side * (frames + 1) + slot]
                weight = jnp.exp2(block * scale - shift)
                total += jnp.sum(weight, axis=0, keepdims=True)
                weights.append(weight.astype(jnp.bfloat16))
            weighted += jnp.dot(
                values[h % 2, side],
                jnp.concatenate(weights, 0),
                preferred_element_type=jnp.float32,
            )
        safe = jnp.maximum(total, 1.0)
        share = weighted * (1.0 / safe)
        lse = peak + jnp.log(safe) * LOG2E
        return [
            (share[:, at * toks : (at + 1) * toks], lse[:, at * toks : (at + 1) * toks])
            for at in range(2)
        ]

    def far_copies(h):
        inner = []
        across = []
        beside = device_of(jnp.clip(group + inward, 0, members - 1))
        for i in range(size):
            dest = device_of(other * size + i)
            src = far_out.at[h, i]
            inner.append(remote(src, relay_in.at[h, i], far_sem.at[h, i], relay_recv.at[h, i], beside))
            across.append(remote(src, far_in.at[h], far_sem.at[h, i], far_recv.at[h, 0], dest))
            across.append(
                remote(
                    far_lse_out.at[h],
                    far_lse_in.at[h],
                    far_sem.at[h, size + i],
                    far_recv.at[h, 1],
                    dest,
                )
            )
        inner.append(
            remote(
                far_lse_out.at[h],
                relay_lse_in.at[h],
                far_sem.at[h, size],
                relay_recv.at[h, size],
                beside,
            )
        )
        return inner, across

    def send_far(h):
        inner, across = far_copies(h)

        @pl.when(jnp.logical_not(innermost))
        def _():
            for copy in inner:
                copy.start()

        @pl.when(innermost)
        def _():
            for copy in across:
                copy.start()

    def merge(h):
        for copy in far_copies(h)[0]:
            copy.wait_recv()
        for i in range(size):
            own = held_lse[i : i + 1, :]
            theirs = relay_lse_in[h, i : i + 1, :]
            top = jnp.maximum(own, theirs)
            own_factor = jnp.exp2(own - top)
            their_factor = jnp.exp2(theirs - top)
            both = own_factor + their_factor
            inverse = 1.0 / both
            far_out[h, i] = (
                held[i] * (own_factor * inverse)
                + relay_in[h, i].astype(jnp.float32) * (their_factor * inverse)
            ).astype(jnp.bfloat16)
            far_lse_out[h, i : i + 1, :] = top + jnp.log(both) * LOG2E
        send_far(h)

    def near_copies(h):
        copies = []
        for d in range(1, size):
            to = lax.rem(place + d, size)
            dest = device_of(half * size + to)
            copies.append(
                remote(
                    near_out.at[h, to],
                    near_in.at[h, size - d],
                    near_sem.at[h, 0, d],
                    near_sem.at[h, 1, size - d],
                    dest,
                )
            )
            copies.append(
                remote(
                    near_lse_out.at[h],
                    near_lse_in.at[h, size - d],
                    near_sem.at[h, 2, d],
                    near_sem.at[h, 3, size - d],
                    dest,
                )
            )
        return copies

    def finish(h):
        for copy in near_copies(h):
            copy.wait_recv()
        far_copies(h)[1][0].wait_recv()
        far_copies(h)[1][1].wait_recv()
        mine = pl.ds(place, 1)
        rows = [near_lse_out[h, mine, :], far_lse_in[h, mine, :]]
        parts = [near_out[h, place], far_in[h]]
        for d in range(1, size):
            rows.append(near_lse_in[h, d, mine, :])
            parts.append(near_in[h, d])
        top = functools.reduce(jnp.maximum, rows)
        factors = [jnp.exp2(row - top) for row in rows]
        inverse = 1.0 / functools.reduce(jnp.add, factors)
        summed = functools.reduce(
            jnp.add,
            [
                part.astype(jnp.float32) * (factor * inverse)
                for part, factor in zip(parts, factors)
            ],
        )
        out_ref[:, h * dim : (h + 1) * dim] = summed.T.astype(out_ref.dtype)

    pass_on(0)
    for h in range(heads):
        for copy in local[h]:
            copy.wait()
        for j in range(frames + 1):
            forward[h, j].wait_recv()
        for side in range(2):
            for slot in range(frames + 1):
                values[h % 2, side, :, slot * toks : (slot + 1) * toks] = kv[
                    side, h, slot, :, dim:
                ].T
        for i in range(size):
            member = other * size + i
            pl.when(jnp.logical_not(jnp.logical_and(passes, member == end_from)))(
                functools.partial(query_wait, h, member)
            )
        for pair in range(size // 2):
            for at, (share, lse) in enumerate(compute(h, other * size + 2 * pair)):
                i = 2 * pair + at
                held[i] = share
                held_lse[i : i + 1, :] = lse

        @pl.when(outermost)
        def _():
            for i in range(size):
                far_out[h, i] = held[i].astype(jnp.bfloat16)
                far_lse_out[h, i : i + 1, :] = held_lse[i : i + 1, :]
            send_far(h)

        if h + 1 < heads:
            pass_on(h + 1)
        for d in range(1, size):
            query_wait(h, half * size + lax.rem(place + d, size))
        for pair in range(size // 2):
            for at, (share, lse) in enumerate(compute(h, half * size + 2 * pair)):
                i = 2 * pair + at
                near_out[h, i] = share.astype(jnp.bfloat16)
                near_lse_out[h, i : i + 1, :] = lse
        for copy in near_copies(h):
            copy.start()
        pl.when(jnp.logical_not(outermost))(functools.partial(merge, h))
        if h > 0:
            finish(h - 1)
    finish(heads - 1)

    for h in range(heads):
        for j in range(1, frames):
            past_in[h, j].wait_send()
        for j in range(1, members):
            pl.when(query_out[h, j][0])(query_out[h, j][1].wait_send)
        pl.when(passes)(query_on[h].wait_send)
        for j in range(frames + 1):
            forward[h, j].wait_send()
        for copy in near_copies(h):
            copy.wait_send()

        @pl.when(jnp.logical_not(innermost))
        def _():
            for copy in far_copies(h)[0]:
                copy.wait_send()

        @pl.when(innermost)
        def _():
            for copy in far_copies(h)[1]:
                copy.wait_send()


def body(qkv_now, past_cache, frame_rank, frame_depth, tile_lists):
    toks, heads, width = qkv_now.shape
    dim = width // 3
    frames = lax.axis_size("frame")
    members = lax.axis_size("space") // 2
    past = jnp.transpose(past_cache[0], (1, 0, 2))
    qkv = jnp.transpose(qkv_now, (1, 0, 2))
    size = members // 2
    lse_rows = -(-size // 8) * 8
    dma = pltpu.SemaphoreType.DMA
    smem = pl.BlockSpec(memory_space=pltpu.SMEM)
    return pl.pallas_call(
        functools.partial(attend, frames, members, heads),
        out_shape=jax.ShapeDtypeStruct((toks, heads * dim), jnp.bfloat16),
        in_specs=[smem, smem, smem] + [pl.BlockSpec(memory_space=pl.ANY)] * 2,
        out_specs=pl.BlockSpec(memory_space=pltpu.VMEM),
        scratch_shapes=[
            pltpu.VMEM((2, heads, frames + 1, toks, 2 * dim), jnp.bfloat16),
            pltpu.VMEM((heads, members, toks, dim), jnp.bfloat16),
            pltpu.VMEM((2, 2, dim, (frames + 1) * toks), jnp.bfloat16),
            pltpu.VMEM((heads, size, dim, toks), jnp.bfloat16),
            pltpu.VMEM((heads, size, dim, toks), jnp.bfloat16),
            pltpu.VMEM((heads, size, dim, toks), jnp.bfloat16),
            pltpu.VMEM((heads, size, dim, toks), jnp.bfloat16),
            pltpu.VMEM((heads, dim, toks), jnp.bfloat16),
            pltpu.VMEM((heads, lse_rows, toks), jnp.float32),
            pltpu.VMEM((heads, size, lse_rows, toks), jnp.float32),
            pltpu.VMEM((heads, lse_rows, toks), jnp.float32),
            pltpu.VMEM((heads, lse_rows, toks), jnp.float32),
            pltpu.VMEM((heads, lse_rows, toks), jnp.float32),
            pltpu.VMEM((size, dim, toks), jnp.float32),
            pltpu.VMEM((lse_rows, toks), jnp.float32),
            dma((heads, 3)),
            dma((heads, frames)),
            dma((heads, frames)),
            dma((heads, frames + 1)),
            dma((heads, frames + 1)),
            dma((heads, members)),
            dma((heads, members)),
            dma((heads, 4, size)),
            dma((heads, 2 * size)),
            dma((heads, size + 1)),
            dma((heads, 2)),
        ],
        compiler_params=pltpu.CompilerParams(
            collective_id=0, has_side_effects=True, vmem_limit_bytes=48 * 1024 * 1024
        ),
    )(frame_rank, frame_depth, tile_lists, past, qkv)


def solution(mesh):
    in_specs = (P("space", "frame", None), P("frame", "space", None, None), P(), P(), P())
    out_specs = P("space", "frame")
    return jax.shard_map(body, mesh=mesh, in_specs=in_specs, out_specs=out_specs, check_vma=False)
```

```python
import functools
import math

import jax
import jax.numpy as jnp
from jax import lax
from jax.experimental import pallas as pl
from jax.experimental.pallas import tpu as pltpu
from jax.sharding import PartitionSpec as P

HIDDEN = -1e30
FLOOR = -1e29
MESH = pl.DeviceIdType.MESH
LOG2E = math.log2(math.e)


def attend(
    frames,
    members,
    heads,
    rank_ref,
    depth_ref,
    lists_ref,
    past_ref,
    qkv_ref,
    out_ref,
    early_kv,
    late_kv,
    queries,
    early_values,
    late_values,
    bias_rows,
    part_sum,
    part_stat,
    share_out,
    share_in,
    lse_out,
    lse_in,
    local_sem,
    past_send,
    past_recv,
    fwd_send,
    fwd_recv,
    query_send,
    query_recv,
    share_send,
    share_recv,
    lse_send,
    lse_recv,
):
    toks = past_ref.shape[1]
    dim = past_ref.shape[2] // 2
    scale = LOG2E / math.sqrt(dim)
    fi = lax.axis_index("frame")
    si = lax.axis_index("space")
    group = si // 2
    core = si % 2
    beside = group * 2 + 1 - core
    peer = (fi, beside)
    size = members // 2
    half = group // size
    place = group - half * size
    passes = jnp.logical_or(group == 1, group == members - 2)
    end_from = jnp.where(group == 1, members - 1, 0)
    end_to = members - 1 - end_from

    def frame_at(slot):
        return lax.rem(fi + slot, frames)

    def device_of(member):
        return (fi, member * 2 + core)

    def remote(src, dst, send_sem, recv_sem, device):
        return pltpu.make_async_remote_copy(
            src_ref=src,
            dst_ref=dst,
            send_sem=send_sem,
            recv_sem=recv_sem,
            device_id=device,
            device_id_type=MESH,
        )

    def own_past(h):
        return past_ref.at[fi * heads + h]

    def own_now(h):
        return qkv_ref.at[h, :, pl.ds(dim, 2 * dim)]

    def own_query(h):
        return qkv_ref.at[h, :, pl.ds(0, dim)]

    local = [
        [
            pltpu.make_async_copy(own_past(h), early_kv.at[0, h, 0], local_sem.at[h, 0]),
            pltpu.make_async_copy(own_now(h), early_kv.at[0, h, 1], local_sem.at[h, 1]),
            pltpu.make_async_copy(own_query(h), queries.at[h, group], local_sem.at[h, 2]),
        ]
        for h in range(heads)
    ]
    for copies in local:
        for copy in copies:
            copy.start()

    def past_copy(h, j):
        to = frame_at(frames - j)
        return remote(
            past_ref.at[to * heads + h],
            late_kv.at[0, h, j - 1],
            past_send.at[h, j],
            past_recv.at[h, j],
            (to, si),
        )

    def early_forward(h, j):
        return remote(
            (own_past, own_now)[j](h),
            early_kv.at[1, h, j],
            fwd_send.at[h, frames - 1 + j],
            fwd_recv.at[h, frames - 1 + j],
            peer,
        )

    def late_forward(h, j):
        return remote(
            late_kv.at[0, h, j],
            late_kv.at[1, h, j],
            fwd_send.at[h, j],
            fwd_recv.at[h, j],
            peer,
        )

    def query_copy(h, j):
        to = lax.rem(group + j, members)
        return jnp.abs(to - group) != members - 1, remote(
            own_query(h),
            queries.at[h, group],
            query_send.at[h, j],
            query_recv.at[h, group],
            device_of(to),
        )

    def query_on(h):
        return remote(
            queries.at[h, end_from],
            queries.at[h, end_from],
            query_send.at[h, 0],
            query_recv.at[h, end_from],
            device_of(end_to),
        )

    def query_wait(h, member):
        remote(
            queries.at[h, member],
            queries.at[h, member],
            query_send.at[h, 0],
            query_recv.at[h, member],
            peer,
        ).wait_recv()

    def start_past(h):
        for j in range(1, frames):
            past_copy(h, j).start()

    def start_query(h):
        for j in range(1, members):
            wanted, copy = query_copy(h, j)
            pl.when(wanted)(copy.start)

    barrier = pltpu.get_barrier_semaphore()
    partners = [(frame_at(j), si) for j in range(1, frames)]
    partners += [device_of(lax.rem(group + j, members)) for j in range(1, members)]
    partners.append(peer)
    for partner in partners:
        pl.semaphore_signal(barrier, inc=1, device_id=partner, device_id_type=MESH)
    pl.semaphore_wait(barrier, len(partners))

    ahead = min(2, heads)
    for h in range(ahead):
        start_past(h)
        start_query(h)
        for j in range(2):
            early_forward(h, j).start()
    for h in range(ahead, heads):
        for j in range(2):
            early_forward(h, j).start()

    lse_out[...] = jnp.zeros_like(lse_out)
    lanes = lax.broadcasted_iota(jnp.int32, (1, 2 * toks), 1)

    def bias_of(key_tile, slot, tile):
        sees = lists_ref[tile, key_tile] > 0
        if slot < frames:
            sees = jnp.logical_and(
                sees, rank_ref[frame_at(slot)] >= frames - depth_ref[tile]
            )
        return jnp.where(sees, 0.0, HIDDEN)

    late_slots = frames - 1
    blocks = [(side, slot) for side in range(2) for slot in (0, frames)]
    blocks += [(side, slot) for side in range(2) for slot in range(1, frames)]
    early_count = 4
    for pair in range(size):
        for at, (side, slot) in enumerate(blocks):
            low, high = (
                bias_of((si, beside)[side], slot, (2 * pair + k) * 2 + core) for k in range(2)
            )
            bias_rows[pair, at : at + 1, :] = jnp.where(lanes < toks, low, high)

    def weigh(keys, query, pair, first, count, peak):
        score = lax.dot_general(
            keys, query, (((1,), (1,)), ((), ())), preferred_element_type=jnp.float32
        )
        parts = [score[at * toks : (at + 1) * toks] for at in range(count)]
        bias = [bias_rows[pair, first + at : first + at + 1, :] for at in range(count)]
        for part, row in zip(parts, bias):
            peak = jnp.maximum(peak, jnp.max(part, axis=0, keepdims=True) * scale + row)
        total = jnp.zeros((1, 2 * toks), jnp.float32)
        weights = []
        for part, row in zip(parts, bias):
            weight = jnp.exp2(part * scale - (peak - row))
            total += jnp.sum(weight, axis=0, keepdims=True)
            weights.append(weight.astype(jnp.bfloat16))
        return peak, total, jnp.concatenate(weights, 0)

    def query_of(h, pair):
        return queries[h, pl.ds(2 * pair, 2)].reshape(2 * toks, dim)

    def early(h, pair):
        keys = early_kv[:, h, :, :, :dim].reshape(4 * toks, dim)
        floor = jnp.full((1, 2 * toks), FLOOR, jnp.float32)
        peak, total, weights = weigh(keys, query_of(h, pair), pair, 0, early_count, floor)
        part_sum[h, pair] = jnp.dot(early_values[...], weights, preferred_element_type=jnp.float32)
        part_stat[h, pair, 0:1, :] = peak
        part_stat[h, pair, 1:2, :] = total

    def share_copy(h, member):
        return remote(
            share_out.at[h, member],
            share_in.at[h, group],
            share_send.at[h, member],
            share_recv.at[h, group],
            device_of(member),
        )

    def late(h, pair):
        keys = late_kv[:, h, :, :, :dim].reshape(2 * late_slots * toks, dim)
        before = part_stat[h, pair, 0:1, :]
        peak, total, weights = weigh(
            keys, query_of(h, pair), pair, early_count, 2 * late_slots, before
        )
        factor = jnp.exp2(before - peak)
        safe = jnp.maximum(total + part_stat[h, pair, 1:2, :] * factor, 1.0)
        inverse = 1.0 / safe
        weighted = jnp.dot(late_values[...], weights, preferred_element_type=jnp.float32)
        share = (weighted * inverse + part_sum[h, pair] * (factor * inverse)).astype(jnp.bfloat16)
        lse = peak + jnp.log(safe) * LOG2E
        for at in range(2):
            member = 2 * pair + at
            share_out[h, member] = share[:, at * toks : (at + 1) * toks]
            lse_out[member, h : h + 1, :] = lse[:, at * toks : (at + 1) * toks]
            pl.when(member != group)(share_copy(h, member).start)

    def early_head(h):
        for copy in local[h]:
            copy.wait()
        for j in range(2):
            early_forward(h, j).wait_recv()
        for side in range(2):
            for j in range(2):
                at = (2 * side + j) * toks
                early_values[:, at : at + toks] = early_kv[side, h, j, :, dim:].T
        for d in range(1, size):
            query_wait(h, half * size + lax.rem(place + d, size))
        for k in range(size // 2):
            early(h, half * (size // 2) + k)

        @pl.when(passes)
        def _():
            query_wait(h, end_from)
            query_on(h).start()

        for i in range(size):
            member = (1 - half) * size + i
            pl.when(jnp.logical_not(jnp.logical_and(passes, member == end_from)))(
                functools.partial(query_wait, h, member)
            )
        if h + ahead < heads:
            start_query(h + ahead)
        for k in range(size // 2):
            early(h, (1 - half) * (size // 2) + k)

    def pass_on(h):
        for j in range(1, frames):
            past_copy(h, j).wait_recv()
            late_forward(h, j - 1).start()
        if h + ahead < heads:
            start_past(h + ahead)

    def late_head(h):
        for j in range(late_slots):
            late_forward(h, j).wait_recv()
        for side in range(2):
            for j in range(late_slots):
                at = (side * late_slots + j) * toks
                late_values[:, at : at + toks] = late_kv[side, h, j, :, dim:].T
        for part in (1 - half, half):
            for k in range(size // 2):
                late(h, part * (size // 2) + k)

    passed = 0
    for h in range(heads):
        early_head(h)
        if 1 <= h <= heads - 2:
            pass_on(passed)
            passed += 1
    for h in range(heads):
        while passed <= h:
            pass_on(passed)
            passed += 1
        late_head(h)
        if passed < heads:
            pass_on(passed)
            passed += 1

    def lse_copy(j):
        member = lax.rem(group + j, members)
        return remote(
            lse_out.at[member],
            lse_in.at[group],
            lse_send.at[member],
            lse_recv.at[group],
            device_of(member),
        )

    for j in range(1, members):
        lse_copy(j).start()

    def arrived(j):
        member = lax.rem(group + j, members)
        return member, remote(
            lse_out.at[member], lse_in.at[member], lse_send.at[member], lse_recv.at[member], peer
        )

    for j in range(1, members):
        arrived(j)[1].wait_recv()
    for h in range(heads):
        rows = [lse_out[group, h : h + 1, :]]
        parts = [share_out[h, group]]
        for j in range(1, members):
            member = lax.rem(group + j, members)
            remote(
                share_out.at[h, member],
                share_in.at[h, member],
                share_send.at[h, member],
                share_recv.at[h, member],
                peer,
            ).wait_recv()
            rows.append(lse_in[member, h : h + 1, :])
            parts.append(share_in[h, member])
        top = functools.reduce(jnp.maximum, rows)
        factors = [jnp.exp2(row - top) for row in rows]
        inverse = 1.0 / functools.reduce(jnp.add, factors)
        summed = functools.reduce(
            jnp.add,
            [
                part.astype(jnp.float32) * (factor * inverse)
                for part, factor in zip(parts, factors)
            ],
        )
        out_ref[:, h * dim : (h + 1) * dim] = summed.T.astype(out_ref.dtype)

    for h in range(heads):
        for j in range(1, frames):
            past_copy(h, j).wait_send()
            late_forward(h, j - 1).wait_send()
        for j in range(2):
            early_forward(h, j).wait_send()
        for j in range(1, members):
            wanted, copy = query_copy(h, j)
            pl.when(wanted)(copy.wait_send)
            share_copy(h, lax.rem(group + j, members)).wait_send()
        pl.when(passes)(query_on(h).wait_send)
    for j in range(1, members):
        lse_copy(j).wait_send()


def body(qkv_now, past_cache, frame_rank, frame_depth, tile_lists):
    toks, heads, width = qkv_now.shape
    dim = width // 3
    frames = lax.axis_size("frame")
    members = lax.axis_size("space") // 2
    past = jnp.transpose(past_cache[0], (1, 0, 2))
    qkv = jnp.transpose(qkv_now, (1, 0, 2))
    lse_rows = -(-heads // 8) * 8
    bias_count = -(-2 * (frames + 1) // 8) * 8
    half = members // 2
    dma = pltpu.SemaphoreType.DMA
    smem = pl.BlockSpec(memory_space=pltpu.SMEM)
    return pl.pallas_call(
        functools.partial(attend, frames, members, heads),
        out_shape=jax.ShapeDtypeStruct((toks, heads * dim), jnp.bfloat16),
        in_specs=[smem, smem, smem] + [pl.BlockSpec(memory_space=pl.ANY)] * 2,
        out_specs=pl.BlockSpec(memory_space=pltpu.VMEM),
        scratch_shapes=[
            pltpu.VMEM((2, heads, 2, toks, 2 * dim), jnp.bfloat16),
            pltpu.VMEM((2, heads, frames - 1, toks, 2 * dim), jnp.bfloat16),
            pltpu.VMEM((heads, members, toks, dim), jnp.bfloat16),
            pltpu.VMEM((dim, 4 * toks), jnp.bfloat16),
            pltpu.VMEM((dim, 2 * (frames - 1) * toks), jnp.bfloat16),
            pltpu.VMEM((half, bias_count, 2 * toks), jnp.float32),
            pltpu.VMEM((heads, half, dim, 2 * toks), jnp.float32),
            pltpu.VMEM((heads, half, 8, 2 * toks), jnp.float32),
            pltpu.VMEM((heads, members, dim, toks), jnp.bfloat16),
            pltpu.VMEM((heads, members, dim, toks), jnp.bfloat16),
            pltpu.VMEM((members, lse_rows, toks), jnp.float32),
            pltpu.VMEM((members, lse_rows, toks), jnp.float32),
            dma((heads, 3)),
            dma((heads, frames)),
            dma((heads, frames)),
            dma((heads, frames + 1)),
            dma((heads, frames + 1)),
            dma((heads, members)),
            dma((heads, members)),
            dma((heads, members)),
            dma((heads, members)),
            dma((members,)),
            dma((members,)),
        ],
        compiler_params=pltpu.CompilerParams(
            collective_id=0, has_side_effects=True, vmem_limit_bytes=48 * 1024 * 1024
        ),
    )(frame_rank, frame_depth, tile_lists, past, qkv)


def solution(mesh):
    in_specs = (P("space", "frame", None), P("frame", "space", None, None), P(), P(), P())
    out_specs = P("space", "frame")
    return jax.shard_map(body, mesh=mesh, in_specs=in_specs, out_specs=out_specs, check_vma=False)
```

```python
import functools
import math

import jax
import jax.numpy as jnp
from jax import lax
from jax.experimental import pallas as pl
from jax.experimental.pallas import tpu as pltpu
from jax.sharding import PartitionSpec as P

HIDDEN = -1e30
FLOOR = -1e29
MESH = pl.DeviceIdType.MESH
LOG2E = math.log2(math.e)


def attend(
    frames,
    members,
    heads,
    rank_ref,
    depth_ref,
    lists_ref,
    past_ref,
    qkv_ref,
    out_ref,
    early_kv,
    late_kv,
    queries,
    early_values,
    late_values,
    bias_rows,
    part_sum,
    part_stat,
    share_out,
    share_in,
    lse_out,
    lse_in,
    local_sem,
    past_send,
    past_recv,
    fwd_send,
    fwd_recv,
    query_send,
    query_recv,
    share_send,
    share_recv,
    lse_send,
    lse_recv,
):
    toks = past_ref.shape[1]
    dim = past_ref.shape[2] // 2
    scale = LOG2E / math.sqrt(dim)
    fi = lax.axis_index("frame")
    si = lax.axis_index("space")
    group = si // 2
    core = si % 2
    beside = group * 2 + 1 - core
    peer = (fi, beside)
    size = members // 2
    half = group // size
    place = group - half * size
    passes = jnp.logical_or(group == 1, group == members - 2)
    end_from = jnp.where(group == 1, members - 1, 0)
    end_to = members - 1 - end_from

    def frame_at(slot):
        return lax.rem(fi + slot, frames)

    def device_of(member):
        return (fi, member * 2 + core)

    def remote(src, dst, send_sem, recv_sem, device):
        return pltpu.make_async_remote_copy(
            src_ref=src,
            dst_ref=dst,
            send_sem=send_sem,
            recv_sem=recv_sem,
            device_id=device,
            device_id_type=MESH,
        )

    def own_past(h):
        return past_ref.at[fi * heads + h]

    def own_now(h):
        return qkv_ref.at[h, :, pl.ds(dim, 2 * dim)]

    def own_query(h):
        return qkv_ref.at[h, :, pl.ds(0, dim)]

    def local_copies(h):
        return [
            pltpu.make_async_copy(own_past(h), early_kv.at[0, h, 0], local_sem.at[h, 0]),
            pltpu.make_async_copy(own_now(h), early_kv.at[0, h, 1], local_sem.at[h, 1]),
            pltpu.make_async_copy(own_query(h), queries.at[h, group], local_sem.at[h, 2]),
        ]

    def each(count, step):
        lax.fori_loop(0, count, lambda at, carry: (step(at), carry)[1], 0)

    def past_copy(h, j):
        to = frame_at(frames - j)
        return remote(
            past_ref.at[to * heads + h],
            late_kv.at[0, h, j - 1],
            past_send.at[h, j],
            past_recv.at[h, j],
            (to, si),
        )

    def early_forward(h, j):
        return remote(
            (own_past, own_now)[j](h),
            early_kv.at[1, h, j],
            fwd_send.at[h, frames - 1 + j],
            fwd_recv.at[h, frames - 1 + j],
            peer,
        )

    def late_forward(h, j):
        return remote(
            late_kv.at[0, h, j],
            late_kv.at[1, h, j],
            fwd_send.at[h, j],
            fwd_recv.at[h, j],
            peer,
        )

    def query_copy(h, j):
        to = lax.rem(group + j, members)
        return jnp.abs(to - group) != members - 1, remote(
            own_query(h),
            queries.at[h, group],
            query_send.at[h, j],
            query_recv.at[h, group],
            device_of(to),
        )

    def query_on(h):
        return remote(
            queries.at[h, end_from],
            queries.at[h, end_from],
            query_send.at[h, 0],
            query_recv.at[h, end_from],
            device_of(end_to),
        )

    def query_wait(h, member):
        remote(
            queries.at[h, member],
            queries.at[h, member],
            query_send.at[h, 0],
            query_recv.at[h, member],
            peer,
        ).wait_recv()

    def start_past(h):
        for j in range(1, frames):
            past_copy(h, j).start()

    def start_query(h):
        for j in range(1, members):
            wanted, copy = query_copy(h, j)
            pl.when(wanted)(copy.start)

    barrier = pltpu.get_barrier_semaphore()
    partners = [(frame_at(j), si) for j in range(1, frames)]
    partners += [device_of(lax.rem(group + j, members)) for j in range(1, members)]
    partners.append(peer)
    for partner in partners:
        pl.semaphore_signal(barrier, inc=1, device_id=partner, device_id_type=MESH)
    pl.semaphore_wait(barrier, len(partners))

    def start_head(h):
        start_past(h)
        start_query(h)
        for j in range(2):
            early_forward(h, j).start()
        for copy in local_copies(h):
            copy.start()

    each(heads, start_head)
    lse_out[...] = jnp.zeros_like(lse_out)
    lanes = lax.broadcasted_iota(jnp.int32, (1, 2 * toks), 1)

    def bias_of(key_tile, slot, tile):
        sees = lists_ref[tile, key_tile] > 0
        if slot < frames:
            sees = jnp.logical_and(
                sees, rank_ref[frame_at(slot)] >= frames - depth_ref[tile]
            )
        return jnp.where(sees, 0.0, HIDDEN)

    late_slots = frames - 1
    blocks = [(side, slot) for side in range(2) for slot in (0, frames)]
    blocks += [(side, slot) for side in range(2) for slot in range(1, frames)]
    early_count = 4

    def set_bias(pair):
        for at, (side, slot) in enumerate(blocks):
            low, high = (
                bias_of((si, beside)[side], slot, (2 * pair + k) * 2 + core) for k in range(2)
            )
            bias_rows[pair, at : at + 1, :] = jnp.where(lanes < toks, low, high)

    each(size, set_bias)

    def weigh(keys, query, pair, first, count, peak):
        score = lax.dot_general(
            keys, query, (((1,), (1,)), ((), ())), preferred_element_type=jnp.float32
        )
        parts = [score[at * toks : (at + 1) * toks] for at in range(count)]
        bias = [bias_rows[pair, first + at : first + at + 1, :] for at in range(count)]
        for part, row in zip(parts, bias):
            peak = jnp.maximum(peak, jnp.max(part, axis=0, keepdims=True) * scale + row)
        total = jnp.zeros((1, 2 * toks), jnp.float32)
        weights = []
        for part, row in zip(parts, bias):
            weight = jnp.exp2(part * scale - (peak - row))
            total += jnp.sum(weight, axis=0, keepdims=True)
            weights.append(weight.astype(jnp.bfloat16))
        return peak, total, jnp.concatenate(weights, 0)

    def query_of(h, pair):
        return queries[h, pl.ds(2 * pair, 2)].reshape(2 * toks, dim)

    def early(h, pair):
        keys = early_kv[:, h, :, :, :dim].reshape(4 * toks, dim)
        floor = jnp.full((1, 2 * toks), FLOOR, jnp.float32)
        peak, total, weights = weigh(keys, query_of(h, pair), pair, 0, early_count, floor)
        part_sum[h, pair] = jnp.dot(early_values[...], weights, preferred_element_type=jnp.float32)
        part_stat[h, pair, 0:1, :] = peak
        part_stat[h, pair, 1:2, :] = total

    def share_copy(h, member):
        return remote(
            share_out.at[h, member],
            share_in.at[h, group],
            share_send.at[h, member],
            share_recv.at[h, group],
            device_of(member),
        )

    def late(h, pair):
        keys = late_kv[:, h, :, :, :dim].reshape(2 * late_slots * toks, dim)
        before = part_stat[h, pair, 0:1, :]
        peak, total, weights = weigh(
            keys, query_of(h, pair), pair, early_count, 2 * late_slots, before
        )
        factor = jnp.exp2(before - peak)
        safe = jnp.maximum(total + part_stat[h, pair, 1:2, :] * factor, 1.0)
        inverse = 1.0 / safe
        weighted = jnp.dot(late_values[...], weights, preferred_element_type=jnp.float32)
        share = (weighted * inverse + part_sum[h, pair] * (factor * inverse)).astype(jnp.bfloat16)
        lse = peak + jnp.log(safe) * LOG2E
        for at in range(2):
            member = 2 * pair + at
            share_out[h, member] = share[:, at * toks : (at + 1) * toks]
            lse_out[member, pl.ds(h, 1), :] = lse[:, at * toks : (at + 1) * toks]
            pl.when(member != group)(share_copy(h, member).start)

    def early_head(h):
        for copy in local_copies(h):
            copy.wait()
        for j in range(2):
            early_forward(h, j).wait_recv()
        for side in range(2):
            for j in range(2):
                at = (2 * side + j) * toks
                early_values[:, at : at + toks] = early_kv[side, h, j, :, dim:].T

        def step(k):
            pair = lax.rem(half * (size // 2) + k, size)
            for at in range(2):
                member = 2 * pair + at
                pl.when(member != group)(functools.partial(query_wait, h, member))

                @pl.when(jnp.logical_and(passes, member == end_from))
                def _():
                    query_on(h).start()

            early(h, pair)

        each(size, step)

    def pass_on(h):
        for j in range(1, frames):
            past_copy(h, j).wait_recv()
            late_forward(h, j - 1).start()

    def late_head(h):
        for j in range(late_slots):
            late_forward(h, j).wait_recv()
        for side in range(2):
            for j in range(late_slots):
                at = (side * late_slots + j) * toks
                late_values[:, at : at + toks] = late_kv[side, h, j, :, dim:].T

        def step(k):
            late(h, lax.rem((1 - half) * (size // 2) + k, size))

            @pl.when(jnp.logical_and(k == 0, h + 1 < heads))
            def _():
                pass_on(h + 1)

        each(size, step)

    each(heads, early_head)
    pass_on(0)
    each(heads, late_head)

    def lse_copy(j):
        member = lax.rem(group + j, members)
        return remote(
            lse_out.at[member],
            lse_in.at[group],
            lse_send.at[member],
            lse_recv.at[group],
            device_of(member),
        )

    for j in range(1, members):
        lse_copy(j).start()

    def arrived(j):
        member = lax.rem(group + j, members)
        return member, remote(
            lse_out.at[member], lse_in.at[member], lse_send.at[member], lse_recv.at[member], peer
        )

    for j in range(1, members):
        arrived(j)[1].wait_recv()
    def finish(h):
        row = pl.ds(h, 1)
        rows = [lse_out[group, row, :]]
        parts = [share_out[h, group]]
        for j in range(1, members):
            member = lax.rem(group + j, members)
            remote(
                share_out.at[h, member],
                share_in.at[h, member],
                share_send.at[h, member],
                share_recv.at[h, member],
                peer,
            ).wait_recv()
            rows.append(lse_in[member, row, :])
            parts.append(share_in[h, member])
        top = functools.reduce(jnp.maximum, rows)
        factors = [jnp.exp2(row - top) for row in rows]
        inverse = 1.0 / functools.reduce(jnp.add, factors)
        summed = functools.reduce(
            jnp.add,
            [
                part.astype(jnp.float32) * (factor * inverse)
                for part, factor in zip(parts, factors)
            ],
        )
        out_ref[:, pl.ds(pl.multiple_of(h * dim, dim), dim)] = summed.T.astype(out_ref.dtype)

    each(heads, finish)

    def sent(h):
        for j in range(1, frames):
            past_copy(h, j).wait_send()
            late_forward(h, j - 1).wait_send()
        for j in range(2):
            early_forward(h, j).wait_send()
        for j in range(1, members):
            wanted, copy = query_copy(h, j)
            pl.when(wanted)(copy.wait_send)
            share_copy(h, lax.rem(group + j, members)).wait_send()
        pl.when(passes)(query_on(h).wait_send)

    each(heads, sent)
    for j in range(1, members):
        lse_copy(j).wait_send()


def body(qkv_now, past_cache, frame_rank, frame_depth, tile_lists):
    toks, heads, width = qkv_now.shape
    dim = width // 3
    frames = lax.axis_size("frame")
    members = lax.axis_size("space") // 2
    past = jnp.transpose(past_cache[0], (1, 0, 2))
    qkv = jnp.transpose(qkv_now, (1, 0, 2))
    lse_rows = -(-heads // 8) * 8
    bias_count = -(-2 * (frames + 1) // 8) * 8
    half = members // 2
    dma = pltpu.SemaphoreType.DMA
    smem = pl.BlockSpec(memory_space=pltpu.SMEM)
    return pl.pallas_call(
        functools.partial(attend, frames, members, heads),
        out_shape=jax.ShapeDtypeStruct((toks, heads * dim), jnp.bfloat16),
        in_specs=[smem, smem, smem] + [pl.BlockSpec(memory_space=pl.ANY)] * 2,
        out_specs=pl.BlockSpec(memory_space=pltpu.VMEM),
        scratch_shapes=[
            pltpu.VMEM((2, heads, 2, toks, 2 * dim), jnp.bfloat16),
            pltpu.VMEM((2, heads, frames - 1, toks, 2 * dim), jnp.bfloat16),
            pltpu.VMEM((heads, members, toks, dim), jnp.bfloat16),
            pltpu.VMEM((dim, 4 * toks), jnp.bfloat16),
            pltpu.VMEM((dim, 2 * (frames - 1) * toks), jnp.bfloat16),
            pltpu.VMEM((half, bias_count, 2 * toks), jnp.float32),
            pltpu.VMEM((heads, half, dim, 2 * toks), jnp.float32),
            pltpu.VMEM((heads, half, 8, 2 * toks), jnp.float32),
            pltpu.VMEM((heads, members, dim, toks), jnp.bfloat16),
            pltpu.VMEM((heads, members, dim, toks), jnp.bfloat16),
            pltpu.VMEM((members, lse_rows, toks), jnp.float32),
            pltpu.VMEM((members, lse_rows, toks), jnp.float32),
            dma((heads, 3)),
            dma((heads, frames)),
            dma((heads, frames)),
            dma((heads, frames + 1)),
            dma((heads, frames + 1)),
            dma((heads, members)),
            dma((heads, members)),
            dma((heads, members)),
            dma((heads, members)),
            dma((members,)),
            dma((members,)),
        ],
        compiler_params=pltpu.CompilerParams(
            collective_id=0, has_side_effects=True, vmem_limit_bytes=48 * 1024 * 1024
        ),
    )(frame_rank, frame_depth, tile_lists, past, qkv)


def solution(mesh):
    in_specs = (P("space", "frame", None), P("frame", "space", None, None), P(), P(), P())
    out_specs = P("space", "frame")
    return jax.shard_map(body, mesh=mesh, in_specs=in_specs, out_specs=out_specs, check_vma=False)
```

```python
import functools
import math

import jax
import jax.numpy as jnp
from jax import lax
from jax.experimental import pallas as pl
from jax.experimental.pallas import tpu as pltpu
from jax.sharding import PartitionSpec as P

HIDDEN = -1e30
FLOOR = -1e29
MESH = pl.DeviceIdType.MESH
LOG2E = math.log2(math.e)


def attend(
    frames,
    members,
    heads,
    rank_ref,
    depth_ref,
    lists_ref,
    past_ref,
    qkv_ref,
    out_ref,
    kv,
    queries,
    bias,
    lse_cols,
    share_out,
    share_in,
    lse_out,
    lse_in,
    local_sem,
    past_send,
    past_recv,
    fwd_send,
    fwd_recv,
    query_send,
    query_recv,
    share_send,
    share_recv,
    lse_send,
    lse_recv,
):
    toks = past_ref.shape[1]
    dim = past_ref.shape[2] // 2
    scale = LOG2E / math.sqrt(dim)
    fi = lax.axis_index("frame")
    si = lax.axis_index("space")
    group = si // 2
    core = si % 2
    beside = group * 2 + 1 - core
    peer = (fi, beside)
    size = members // 2
    half = group // size
    place = group - half * size
    passes = jnp.logical_or(group == 1, group == members - 2)
    end_from = jnp.where(group == 1, members - 1, 0)
    end_to = members - 1 - end_from

    def frame_at(slot):
        return lax.rem(fi + slot, frames)

    def device_of(member):
        return (fi, member * 2 + core)

    def remote(src, dst, send_sem, recv_sem, device):
        return pltpu.make_async_remote_copy(
            src_ref=src,
            dst_ref=dst,
            send_sem=send_sem,
            recv_sem=recv_sem,
            device_id=device,
            device_id_type=MESH,
        )

    def own_past(h):
        return past_ref.at[fi * heads + h]

    def own_now(h):
        return qkv_ref.at[h, :, pl.ds(dim, 2 * dim)]

    def own_query(h):
        return qkv_ref.at[h, :, pl.ds(0, dim)]

    def local_copies(h):
        return [
            pltpu.make_async_copy(own_past(h), kv.at[0, h, 0], local_sem.at[h, 0]),
            pltpu.make_async_copy(own_now(h), kv.at[0, h, frames], local_sem.at[h, 1]),
            pltpu.make_async_copy(own_query(h), queries.at[h, group], local_sem.at[h, 2]),
        ]

    def each(count, step):
        lax.fori_loop(0, count, lambda at, carry: (step(at), carry)[1], 0)

    def past_copy(h, j):
        to = frame_at(frames - j)
        return remote(
            past_ref.at[to * heads + h],
            kv.at[0, h, j],
            past_send.at[h, j],
            past_recv.at[h, j],
            (to, si),
        )

    def forward(h, j):
        src = kv.at[0, h, j]
        if j == 0:
            src = own_past(h)
        elif j == frames:
            src = own_now(h)
        return remote(src, kv.at[1, h, j], fwd_send.at[h, j], fwd_recv.at[h, j], peer)

    def query_copy(h, j):
        to = lax.rem(group + j, members)
        return jnp.abs(to - group) != members - 1, remote(
            own_query(h),
            queries.at[h, group],
            query_send.at[h, j],
            query_recv.at[h, group],
            device_of(to),
        )

    def query_on(h):
        return remote(
            queries.at[h, end_from],
            queries.at[h, end_from],
            query_send.at[h, 0],
            query_recv.at[h, end_from],
            device_of(end_to),
        )

    def query_wait(h, member):
        remote(
            queries.at[h, member],
            queries.at[h, member],
            query_send.at[h, 0],
            query_recv.at[h, member],
            peer,
        ).wait_recv()

    def start_past(h):
        for j in range(1, frames):
            past_copy(h, j).start()

    def start_query(h):
        for j in range(1, members):
            wanted, copy = query_copy(h, j)
            pl.when(wanted)(copy.start)

    barrier = pltpu.get_barrier_semaphore()
    partners = [(frame_at(j), si) for j in range(1, frames)]
    partners += [device_of(lax.rem(group + j, members)) for j in range(1, members)]
    partners.append(peer)
    for partner in partners:
        pl.semaphore_signal(barrier, inc=1, device_id=partner, device_id_type=MESH)
    pl.semaphore_wait(barrier, len(partners))

    def start_head(h):
        start_past(h)
        start_query(h)
        for j in (0, frames):
            forward(h, j).start()
        for copy in local_copies(h):
            copy.start()

    each(heads, start_head)
    lse_cols[...] = jnp.zeros_like(lse_cols)
    lanes = lax.broadcasted_iota(jnp.int32, (1, toks), 1)

    def bias_of(key_tile, slot, tile):
        sees = lists_ref[tile, key_tile] > 0
        if slot < frames:
            sees = jnp.logical_and(
                sees, rank_ref[frame_at(slot)] >= frames - depth_ref[tile]
            )
        return jnp.where(sees, 0.0, HIDDEN)

    blocks = [(side, slot) for side in range(2) for slot in range(frames + 1)]

    def set_bias(member):
        for at, (side, slot) in enumerate(blocks):
            bias[member, at] = bias_of((si, beside)[side], slot, member * 2 + core)

    each(members, set_bias)

    def share_copy(h, member):
        return remote(
            share_out.at[h, member],
            share_in.at[h, group],
            share_send.at[h, member],
            share_recv.at[h, group],
            device_of(member),
        )

    def unit(h, pair):
        query = queries[h, pl.ds(2 * pair, 2)].reshape(2 * toks, dim)
        keys = kv[:, h, :, :, :dim].reshape(len(blocks) * toks, dim)
        values = kv[:, h, :, :, dim:].reshape(len(blocks) * toks, dim)
        score = lax.dot_general(
            query, keys, (((1,), (1,)), ((), ())), preferred_element_type=jnp.float32
        )
        weights = []
        safes = []
        for at in range(2):
            member = 2 * pair + at
            rows = score[at * toks : (at + 1) * toks]
            parts = [
                rows[:, b * toks : (b + 1) * toks] + bias[member, b] for b in range(len(blocks))
            ]
            peak = jnp.max(functools.reduce(jnp.maximum, parts), axis=1, keepdims=True)
            peak = jnp.maximum(peak, FLOOR) * scale
            parts = [jnp.exp2(part * scale - peak) for part in parts]
            total = jnp.sum(functools.reduce(jnp.add, parts), axis=1, keepdims=True)
            safe = jnp.maximum(total, 1.0)
            safes.append(safe)
            lse = peak + jnp.log(safe) * LOG2E
            lse_cols[member] = jnp.where(lanes == h, lse, lse_cols[member])
            weights.append(jnp.concatenate([part.astype(jnp.bfloat16) for part in parts], 1))
        weighted = jnp.dot(
            jnp.concatenate(weights, 0), values, preferred_element_type=jnp.float32
        )
        for at in range(2):
            member = 2 * pair + at
            share = weighted[at * toks : (at + 1) * toks] * (1.0 / safes[at])
            share_out[h, member] = share.astype(jnp.bfloat16)
            pl.when(member != group)(share_copy(h, member).start)

    def pass_on(h):
        for j in range(1, frames):
            past_copy(h, j).wait_recv()
            forward(h, j).start()

    def head(h):
        for copy in local_copies(h):
            copy.wait()
        for j in range(frames + 1):
            forward(h, j).wait_recv()

        def step(k):
            pair = lax.rem((1 - half) * (size // 2) + k, size)
            for at in range(2):
                member = 2 * pair + at
                pl.when(member != group)(functools.partial(query_wait, h, member))

                @pl.when(jnp.logical_and(passes, member == end_from))
                def _():
                    query_on(h).start()

            unit(h, pair)

            @pl.when(jnp.logical_and(k == 0, h + 1 < heads))
            def _():
                pass_on(h + 1)

        each(size, step)

    pass_on(0)
    each(heads, head)

    for member in range(members):
        lse_out[member] = lse_cols[member].T[: lse_out.shape[1]]

    def lse_copy(j):
        member = lax.rem(group + j, members)
        return remote(
            lse_out.at[member],
            lse_in.at[group],
            lse_send.at[member],
            lse_recv.at[group],
            device_of(member),
        )

    for j in range(1, members):
        lse_copy(j).start()

    def arrived(j):
        member = lax.rem(group + j, members)
        return member, remote(
            lse_out.at[member], lse_in.at[member], lse_send.at[member], lse_recv.at[member], peer
        )

    for j in range(1, members):
        arrived(j)[1].wait_recv()
    rows = [lse_out[group]]
    for j in range(1, members):
        rows.append(lse_in[lax.rem(group + j, members)])
    top = functools.reduce(jnp.maximum, rows)
    factors = [jnp.exp2(row - top) for row in rows]
    inverse = 1.0 / functools.reduce(jnp.add, factors)
    columns = [(factor * inverse).T for factor in factors]
    for h in range(heads):
        summed = share_out[h, group].astype(jnp.float32) * columns[0][:, h : h + 1]
        for j in range(1, members):
            member = lax.rem(group + j, members)
            remote(
                share_out.at[h, member],
                share_in.at[h, member],
                share_send.at[h, member],
                share_recv.at[h, member],
                peer,
            ).wait_recv()
            summed += share_in[h, member].astype(jnp.float32) * columns[j][:, h : h + 1]
        out_ref[:, h * dim : (h + 1) * dim] = summed.astype(out_ref.dtype)

    def sent(h):
        for j in range(1, frames):
            past_copy(h, j).wait_send()
        for j in range(frames + 1):
            forward(h, j).wait_send()
        for j in range(1, members):
            wanted, copy = query_copy(h, j)
            pl.when(wanted)(copy.wait_send)
            share_copy(h, lax.rem(group + j, members)).wait_send()
        pl.when(passes)(query_on(h).wait_send)

    each(heads, sent)
    for j in range(1, members):
        lse_copy(j).wait_send()


def body(qkv_now, past_cache, frame_rank, frame_depth, tile_lists):
    toks, heads, width = qkv_now.shape
    dim = width // 3
    frames = lax.axis_size("frame")
    members = lax.axis_size("space") // 2
    past = jnp.transpose(past_cache[0], (1, 0, 2))
    qkv = jnp.transpose(qkv_now, (1, 0, 2))
    lse_rows = -(-heads // 8) * 8
    dma = pltpu.SemaphoreType.DMA
    smem = pl.BlockSpec(memory_space=pltpu.SMEM)
    return pl.pallas_call(
        functools.partial(attend, frames, members, heads),
        out_shape=jax.ShapeDtypeStruct((toks, heads * dim), jnp.bfloat16),
        in_specs=[smem, smem, smem] + [pl.BlockSpec(memory_space=pl.ANY)] * 2,
        out_specs=pl.BlockSpec(memory_space=pltpu.VMEM),
        scratch_shapes=[
            pltpu.VMEM((2, heads, frames + 1, toks, 2 * dim), jnp.bfloat16),
            pltpu.VMEM((heads, members, toks, dim), jnp.bfloat16),
            pltpu.SMEM((members, 2 * (frames + 1)), jnp.float32),
            pltpu.VMEM((members, toks, toks), jnp.float32),
            pltpu.VMEM((heads, members, toks, dim), jnp.bfloat16),
            pltpu.VMEM((heads, members, toks, dim), jnp.bfloat16),
            pltpu.VMEM((members, lse_rows, toks), jnp.float32),
            pltpu.VMEM((members, lse_rows, toks), jnp.float32),
            dma((heads, 3)),
            dma((heads, frames)),
            dma((heads, frames)),
            dma((heads, frames + 1)),
            dma((heads, frames + 1)),
            dma((heads, members)),
            dma((heads, members)),
            dma((heads, members)),
            dma((heads, members)),
            dma((members,)),
            dma((members,)),
        ],
        compiler_params=pltpu.CompilerParams(
            collective_id=0, has_side_effects=True, vmem_limit_bytes=48 * 1024 * 1024
        ),
    )(frame_rank, frame_depth, tile_lists, past, qkv)


def solution(mesh):
    in_specs = (P("space", "frame", None), P("frame", "space", None, None), P(), P(), P())
    out_specs = P("space", "frame")
    return jax.shard_map(body, mesh=mesh, in_specs=in_specs, out_specs=out_specs, check_vma=False)
```

```python
import functools
import math

import jax
import jax.numpy as jnp
from jax import lax
from jax.experimental import pallas as pl
from jax.experimental.pallas import tpu as pltpu
from jax.sharding import PartitionSpec as P

HIDDEN = -1e30
FLOOR = -1e29
MESH = pl.DeviceIdType.MESH
LOG2E = math.log2(math.e)


def attend_by_tile(
    frames,
    members,
    heads,
    rank_ref,
    depth_ref,
    lists_ref,
    past_ref,
    qkv_ref,
    out_ref,
    kv,
    queries,
    bias,
    lse_cols,
    share_out,
    share_in,
    lse_out,
    lse_in,
    local_sem,
    past_send,
    past_recv,
    fwd_send,
    fwd_recv,
    query_send,
    query_recv,
    share_send,
    share_recv,
    lse_send,
    lse_recv,
):
    toks = past_ref.shape[1]
    dim = past_ref.shape[2] // 2
    scale = LOG2E / math.sqrt(dim)
    fi = lax.axis_index("frame")
    si = lax.axis_index("space")
    group = si // 2
    core = si % 2
    beside = group * 2 + 1 - core
    peer = (fi, beside)
    size = members // 2
    half = group // size
    place = group - half * size
    passes = jnp.logical_or(group == 1, group == members - 2)
    end_from = jnp.where(group == 1, members - 1, 0)
    end_to = members - 1 - end_from

    def frame_at(slot):
        return lax.rem(fi + slot, frames)

    def device_of(member):
        return (fi, member * 2 + core)

    def remote(src, dst, send_sem, recv_sem, device):
        return pltpu.make_async_remote_copy(
            src_ref=src,
            dst_ref=dst,
            send_sem=send_sem,
            recv_sem=recv_sem,
            device_id=device,
            device_id_type=MESH,
        )

    def own_past(h):
        return past_ref.at[fi * heads + h]

    def own_now(h):
        return qkv_ref.at[h, :, pl.ds(dim, 2 * dim)]

    def own_query(h):
        return qkv_ref.at[h, :, pl.ds(0, dim)]

    def local_copies(h):
        return [
            pltpu.make_async_copy(own_past(h), kv.at[0, h, 0], local_sem.at[h, 0]),
            pltpu.make_async_copy(own_now(h), kv.at[0, h, frames], local_sem.at[h, 1]),
            pltpu.make_async_copy(own_query(h), queries.at[h, group], local_sem.at[h, 2]),
        ]

    def each(count, step):
        lax.fori_loop(0, count, lambda at, carry: (step(at), carry)[1], 0)

    def past_copy(h, j):
        to = frame_at(frames - j)
        return remote(
            past_ref.at[to * heads + h],
            kv.at[0, h, j],
            past_send.at[h, j],
            past_recv.at[h, j],
            (to, si),
        )

    def forward(h, j):
        src = kv.at[0, h, j]
        if j == 0:
            src = own_past(h)
        elif j == frames:
            src = own_now(h)
        return remote(src, kv.at[1, h, j], fwd_send.at[h, j], fwd_recv.at[h, j], peer)

    def query_copy(h, j):
        to = lax.rem(group + j, members)
        return jnp.abs(to - group) != members - 1, remote(
            own_query(h),
            queries.at[h, group],
            query_send.at[h, j],
            query_recv.at[h, group],
            device_of(to),
        )

    def query_on(h):
        return remote(
            queries.at[h, end_from],
            queries.at[h, end_from],
            query_send.at[h, 0],
            query_recv.at[h, end_from],
            device_of(end_to),
        )

    def query_wait(h, member):
        remote(
            queries.at[h, member],
            queries.at[h, member],
            query_send.at[h, 0],
            query_recv.at[h, member],
            peer,
        ).wait_recv()

    def start_past(h):
        for j in range(1, frames):
            past_copy(h, j).start()

    def start_query(h):
        for j in range(1, members):
            wanted, copy = query_copy(h, j)
            pl.when(wanted)(copy.start)

    barrier = pltpu.get_barrier_semaphore()
    partners = [(frame_at(j), si) for j in range(1, frames)]
    partners += [device_of(lax.rem(group + j, members)) for j in range(1, members)]
    partners.append(peer)
    for partner in partners:
        pl.semaphore_signal(barrier, inc=1, device_id=partner, device_id_type=MESH)
    pl.semaphore_wait(barrier, len(partners))

    def start_head(h):
        start_past(h)
        start_query(h)
        for j in (0, frames):
            forward(h, j).start()
        for copy in local_copies(h):
            copy.start()

    each(heads, start_head)
    lse_cols[...] = jnp.zeros_like(lse_cols)
    lanes = lax.broadcasted_iota(jnp.int32, (1, toks), 1)

    def bias_of(key_tile, slot, tile):
        sees = lists_ref[tile, key_tile] > 0
        if slot < frames:
            sees = jnp.logical_and(
                sees, rank_ref[frame_at(slot)] >= frames - depth_ref[tile]
            )
        return jnp.where(sees, 0.0, HIDDEN)

    blocks = [(side, slot) for side in range(2) for slot in range(frames + 1)]

    def set_bias(member):
        for at, (side, slot) in enumerate(blocks):
            bias[member, at] = bias_of((si, beside)[side], slot, member * 2 + core)

    each(members, set_bias)

    def share_copy(h, member):
        return remote(
            share_out.at[h, member],
            share_in.at[h, group],
            share_send.at[h, member],
            share_recv.at[h, group],
            device_of(member),
        )

    def unit(h, pair):
        query = queries[h, pl.ds(2 * pair, 2)].reshape(2 * toks, dim)
        keys = kv[:, h, :, :, :dim].reshape(len(blocks) * toks, dim)
        values = kv[:, h, :, :, dim:].reshape(len(blocks) * toks, dim)
        score = lax.dot_general(
            query, keys, (((1,), (1,)), ((), ())), preferred_element_type=jnp.float32
        )
        weights = []
        safes = []
        for at in range(2):
            member = 2 * pair + at
            rows = score[at * toks : (at + 1) * toks]
            parts = [
                rows[:, b * toks : (b + 1) * toks] + bias[member, b] for b in range(len(blocks))
            ]
            peak = jnp.max(functools.reduce(jnp.maximum, parts), axis=1, keepdims=True)
            peak = jnp.maximum(peak, FLOOR) * scale
            parts = [jnp.exp2(part * scale - peak) for part in parts]
            total = jnp.sum(functools.reduce(jnp.add, parts), axis=1, keepdims=True)
            safe = jnp.maximum(total, 1.0)
            safes.append(safe)
            lse = peak + jnp.log(safe) * LOG2E
            lse_cols[member] = jnp.where(lanes == h, lse, lse_cols[member])
            weights.append(jnp.concatenate([part.astype(jnp.bfloat16) for part in parts], 1))
        weighted = jnp.dot(
            jnp.concatenate(weights, 0), values, preferred_element_type=jnp.float32
        )
        for at in range(2):
            member = 2 * pair + at
            share = weighted[at * toks : (at + 1) * toks] * (1.0 / safes[at])
            share_out[h, member] = share.astype(jnp.bfloat16)
            pl.when(member != group)(share_copy(h, member).start)

    def pass_on(h):
        for j in range(1, frames):
            past_copy(h, j).wait_recv()
            forward(h, j).start()

    def head(h):
        for copy in local_copies(h):
            copy.wait()
        for j in range(frames + 1):
            forward(h, j).wait_recv()

        def step(k):
            pair = lax.rem((1 - half) * (size // 2) + k, size)
            for at in range(2):
                member = 2 * pair + at
                pl.when(member != group)(functools.partial(query_wait, h, member))

                @pl.when(jnp.logical_and(passes, member == end_from))
                def _():
                    query_on(h).start()

            unit(h, pair)

            @pl.when(jnp.logical_and(k == 0, h + 1 < heads))
            def _():
                pass_on(h + 1)

        each(size, step)

    pass_on(0)
    each(heads, head)

    for member in range(members):
        lse_out[member] = lse_cols[member].T[: lse_out.shape[1]]

    def lse_copy(j):
        member = lax.rem(group + j, members)
        return remote(
            lse_out.at[member],
            lse_in.at[group],
            lse_send.at[member],
            lse_recv.at[group],
            device_of(member),
        )

    for j in range(1, members):
        lse_copy(j).start()

    def arrived(j):
        member = lax.rem(group + j, members)
        return member, remote(
            lse_out.at[member], lse_in.at[member], lse_send.at[member], lse_recv.at[member], peer
        )

    for j in range(1, members):
        arrived(j)[1].wait_recv()
    rows = [lse_out[group]]
    for j in range(1, members):
        rows.append(lse_in[lax.rem(group + j, members)])
    top = functools.reduce(jnp.maximum, rows)
    factors = [jnp.exp2(row - top) for row in rows]
    inverse = 1.0 / functools.reduce(jnp.add, factors)
    columns = [(factor * inverse).T for factor in factors]
    for h in range(heads):
        summed = share_out[h, group].astype(jnp.float32) * columns[0][:, h : h + 1]
        for j in range(1, members):
            member = lax.rem(group + j, members)
            remote(
                share_out.at[h, member],
                share_in.at[h, member],
                share_send.at[h, member],
                share_recv.at[h, member],
                peer,
            ).wait_recv()
            summed += share_in[h, member].astype(jnp.float32) * columns[j][:, h : h + 1]
        out_ref[:, h * dim : (h + 1) * dim] = summed.astype(out_ref.dtype)

    def sent(h):
        for j in range(1, frames):
            past_copy(h, j).wait_send()
        for j in range(frames + 1):
            forward(h, j).wait_send()
        for j in range(1, members):
            wanted, copy = query_copy(h, j)
            pl.when(wanted)(copy.wait_send)
            share_copy(h, lax.rem(group + j, members)).wait_send()
        pl.when(passes)(query_on(h).wait_send)

    each(heads, sent)
    for j in range(1, members):
        lse_copy(j).wait_send()


def call_by_tile(qkv, past, frame_rank, frame_depth, tile_lists):
    heads, toks, width = qkv.shape
    dim = width // 3
    frames = lax.axis_size("frame")
    members = lax.axis_size("space") // 2
    lse_rows = -(-heads // 8) * 8
    dma = pltpu.SemaphoreType.DMA
    smem = pl.BlockSpec(memory_space=pltpu.SMEM)
    return pl.pallas_call(
        functools.partial(attend_by_tile, frames, members, heads),
        out_shape=jax.ShapeDtypeStruct((toks, heads * dim), jnp.bfloat16),
        in_specs=[smem, smem, smem] + [pl.BlockSpec(memory_space=pl.ANY)] * 2,
        out_specs=pl.BlockSpec(memory_space=pltpu.VMEM),
        scratch_shapes=[
            pltpu.VMEM((2, heads, frames + 1, toks, 2 * dim), jnp.bfloat16),
            pltpu.VMEM((heads, members, toks, dim), jnp.bfloat16),
            pltpu.SMEM((members, 2 * (frames + 1)), jnp.float32),
            pltpu.VMEM((members, toks, toks), jnp.float32),
            pltpu.VMEM((heads, members, toks, dim), jnp.bfloat16),
            pltpu.VMEM((heads, members, toks, dim), jnp.bfloat16),
            pltpu.VMEM((members, lse_rows, toks), jnp.float32),
            pltpu.VMEM((members, lse_rows, toks), jnp.float32),
            dma((heads, 3)),
            dma((heads, frames)),
            dma((heads, frames)),
            dma((heads, frames + 1)),
            dma((heads, frames + 1)),
            dma((heads, members)),
            dma((heads, members)),
            dma((heads, members)),
            dma((heads, members)),
            dma((members,)),
            dma((members,)),
        ],
        compiler_params=pltpu.CompilerParams(
            collective_id=0, has_side_effects=True, vmem_limit_bytes=48 * 1024 * 1024
        ),
    )(frame_rank, frame_depth, tile_lists, past, qkv)


def attend_by_head(
    frames,
    members,
    heads,
    rank_ref,
    depth_ref,
    lists_ref,
    past_ref,
    qkv_ref,
    out_ref,
    kv,
    queries,
    bias,
    lse_cols,
    share_out,
    share_in,
    lse_out,
    lse_in,
    local_sem,
    past_send,
    past_recv,
    query_send,
    query_recv,
    share_send,
    share_recv,
    lse_send,
    lse_recv,
):
    toks = past_ref.shape[1]
    dim = past_ref.shape[2] // 2
    own = heads // 2
    tiles = 2 * members
    scale = LOG2E / math.sqrt(dim)
    fi = lax.axis_index("frame")
    si = lax.axis_index("space")
    group = si // 2
    core = si % 2
    peer = (fi, group * 2 + 1 - core)
    half = group // (members // 2)

    def frame_at(slot):
        return lax.rem(fi + slot, frames)

    def core_at(e):
        return core if e == 0 else 1 - core

    def tile_at(j):
        return lax.rem(si + j, tiles)

    def remote(src, dst, send_sem, recv_sem, device):
        return pltpu.make_async_remote_copy(
            src_ref=src,
            dst_ref=dst,
            send_sem=send_sem,
            recv_sem=recv_sem,
            device_id=device,
            device_id_type=MESH,
        )

    def each(count, step):
        lax.fori_loop(0, count, lambda at, carry: (step(at), carry)[1], 0)

    def past_source(h, e, j):
        to = fi if j in (0, frames) else frame_at(frames - j)
        head = core_at(e) * own + h
        if j == frames:
            return to, qkv_ref.at[head, :, pl.ds(dim, 2 * dim)]
        return to, past_ref.at[to * heads + head]

    def query_source(h, to_core):
        return qkv_ref.at[to_core * own + h, :, pl.ds(0, dim)]

    def local_copies(h):
        return [
            pltpu.make_async_copy(past_source(h, 0, 0)[1], kv.at[h, core, 0], local_sem.at[h, 0]),
            pltpu.make_async_copy(
                past_source(h, 0, frames)[1], kv.at[h, core, frames], local_sem.at[h, 1]
            ),
            pltpu.make_async_copy(query_source(h, core), queries.at[h, si], local_sem.at[h, 2]),
        ]

    sent_blocks = [(e, j) for j in range(1, frames) for e in range(2)] + [(1, 0), (1, frames)]

    def past_copy(h, e, j):
        to, src = past_source(h, e, j)
        return remote(
            src,
            kv.at[h, core, j],
            past_send.at[h, e, j],
            past_recv.at[h, core, j],
            (to, group * 2 + core_at(e)),
        )

    def past_wait(h, e, j):
        block = kv.at[h, core_at(e), j]
        remote(block, block, past_send.at[h, e, j], past_recv.at[h, core_at(e), j], peer).wait_recv()

    def query_copy(h, j):
        to = tile_at(j)
        return remote(
            query_source(h, lax.rem(to, 2)),
            queries.at[h, si],
            query_send.at[h, j],
            query_recv.at[h, si],
            (fi, to),
        )

    def query_wait(h, tile):
        block = queries.at[h, tile]
        remote(block, block, query_send.at[h, 0], query_recv.at[h, tile], peer).wait_recv()

    barrier = pltpu.get_barrier_semaphore()
    partners = [(frame_at(j), group * 2 + e) for j in range(1, frames) for e in range(2)]
    partners += [(fi, tile_at(j)) for j in range(1, tiles)]
    for partner in partners:
        pl.semaphore_signal(barrier, inc=1, device_id=partner, device_id_type=MESH)
    pl.semaphore_wait(barrier, len(partners))

    def start_head(h):
        for e, j in sent_blocks:
            past_copy(h, e, j).start()
        for j in range(1, tiles):
            query_copy(h, j).start()
        for copy in local_copies(h):
            copy.start()

    each(own, start_head)

    lse_cols[...] = jnp.zeros_like(lse_cols)
    lanes = lax.broadcasted_iota(jnp.int32, (1, toks), 1)

    def bias_of(key_tile, slot, tile):
        sees = lists_ref[tile, key_tile] > 0
        if slot < frames:
            sees = jnp.logical_and(
                sees, rank_ref[frame_at(slot)] >= frames - depth_ref[tile]
            )
        return jnp.where(sees, 0.0, HIDDEN)

    blocks = [(side, slot) for side in range(2) for slot in range(frames + 1)]

    def set_bias(tile):
        for at, (side, slot) in enumerate(blocks):
            bias[tile, at] = bias_of(group * 2 + side, slot, tile)

    each(tiles, set_bias)

    def share_copy(h, tile):
        return remote(
            share_out.at[h, tile],
            share_in.at[core * own + h, group],
            share_send.at[h, tile],
            share_recv.at[core * own + h, group],
            (fi, tile),
        )

    def unit(h, member):
        query = queries[h, pl.ds(2 * member, 2)].reshape(2 * toks, dim)
        keys = kv[h, :, :, :, :dim].reshape(len(blocks) * toks, dim)
        values = kv[h, :, :, :, dim:].reshape(len(blocks) * toks, dim)
        score = lax.dot_general(
            query, keys, (((1,), (1,)), ((), ())), preferred_element_type=jnp.float32
        )
        weights = []
        safes = []
        for at in range(2):
            tile = 2 * member + at
            rows = score[at * toks : (at + 1) * toks]
            parts = [
                rows[:, b * toks : (b + 1) * toks] + bias[tile, b] for b in range(len(blocks))
            ]
            peak = jnp.max(functools.reduce(jnp.maximum, parts), axis=1, keepdims=True)
            peak = jnp.maximum(peak, FLOOR) * scale
            parts = [jnp.exp2(part * scale - peak) for part in parts]
            total = jnp.sum(functools.reduce(jnp.add, parts), axis=1, keepdims=True)
            safe = jnp.maximum(total, 1.0)
            safes.append(safe)
            lse = peak + jnp.log(safe) * LOG2E
            lse_cols[tile] = jnp.where(lanes == h, lse, lse_cols[tile])
            weights.append(jnp.concatenate([part.astype(jnp.bfloat16) for part in parts], 1))
        weighted = jnp.dot(
            jnp.concatenate(weights, 0), values, preferred_element_type=jnp.float32
        )
        for at in range(2):
            tile = 2 * member + at
            share = weighted[at * toks : (at + 1) * toks] * (1.0 / safes[at])
            share_out[h, tile] = share.astype(jnp.bfloat16)
            pl.when(tile != si)(share_copy(h, tile).start)

    def head(h):
        for copy in local_copies(h):
            copy.wait()
        for e, j in sent_blocks:
            past_wait(h, e, j)

        def step(k):
            member = lax.rem((1 - half) * (members // 2) + k, members)
            for at in range(2):
                tile = 2 * member + at
                pl.when(tile != si)(functools.partial(query_wait, h, tile))
            unit(h, member)

        each(members, step)

    each(own, head)

    for tile in range(tiles):
        lse_out[tile] = lse_cols[tile].T[: lse_out.shape[1]]

    def lse_copy(j):
        tile = tile_at(j)
        return remote(
            lse_out.at[tile],
            lse_in.at[core, group],
            lse_send.at[tile],
            lse_recv.at[core, group],
            (fi, tile),
        )

    for j in range(1, tiles):
        lse_copy(j).start()
    lse_in[core, group] = lse_out[si]
    for h in range(own):
        share_in[core * own + h, group] = share_out[h, si]
    for j in range(1, tiles):
        tile = tile_at(j)
        block = lse_in.at[lax.rem(tile, 2), tile // 2]
        remote(
            block, block, lse_send.at[tile], lse_recv.at[lax.rem(tile, 2), tile // 2], peer
        ).wait_recv()
    for c in range(2):
        rows = [lse_in[c, m] for m in range(members)]
        top = functools.reduce(jnp.maximum, rows)
        factors = [jnp.exp2(row - top) for row in rows]
        inverse = 1.0 / functools.reduce(jnp.add, factors)
        columns = [(factor * inverse).T for factor in factors]
        for h in range(own):
            at = c * own + h
            summed = 0.0
            for m in range(members):
                block = share_in.at[at, m]
                pl.when(2 * m + c != si)(
                    remote(block, block, share_send.at[h, 0], share_recv.at[at, m], peer).wait_recv
                )
                summed += share_in[at, m].astype(jnp.float32) * columns[m][:, h : h + 1]
            out_ref[:, at * dim : (at + 1) * dim] = summed.astype(out_ref.dtype)

    def sent(h):
        for e, j in sent_blocks:
            past_copy(h, e, j).wait_send()
        for j in range(1, tiles):
            query_copy(h, j).wait_send()
            share_copy(h, tile_at(j)).wait_send()

    each(own, sent)
    for j in range(1, tiles):
        lse_copy(j).wait_send()


def call_by_head(qkv, past, frame_rank, frame_depth, tile_lists):
    heads, toks, width = qkv.shape
    dim = width // 3
    frames = lax.axis_size("frame")
    tiles = lax.axis_size("space")
    members = tiles // 2
    own = heads // 2
    lse_rows = -(-own // 8) * 8
    dma = pltpu.SemaphoreType.DMA
    smem = pl.BlockSpec(memory_space=pltpu.SMEM)
    return pl.pallas_call(
        functools.partial(attend_by_head, frames, members, heads),
        out_shape=jax.ShapeDtypeStruct((toks, heads * dim), jnp.bfloat16),
        in_specs=[smem, smem, smem] + [pl.BlockSpec(memory_space=pl.ANY)] * 2,
        out_specs=pl.BlockSpec(memory_space=pltpu.VMEM),
        scratch_shapes=[
            pltpu.VMEM((own, 2, frames + 1, toks, 2 * dim), jnp.bfloat16),
            pltpu.VMEM((own, tiles, toks, dim), jnp.bfloat16),
            pltpu.SMEM((tiles, 2 * (frames + 1)), jnp.float32),
            pltpu.VMEM((tiles, toks, toks), jnp.float32),
            pltpu.VMEM((own, tiles, toks, dim), jnp.bfloat16),
            pltpu.VMEM((heads, members, toks, dim), jnp.bfloat16),
            pltpu.VMEM((tiles, lse_rows, toks), jnp.float32),
            pltpu.VMEM((2, members, lse_rows, toks), jnp.float32),
            dma((own, 3)),
            dma((own, 2, frames + 1)),
            dma((own, 2, frames + 1)),
            dma((own, tiles)),
            dma((own, tiles)),
            dma((own, tiles)),
            dma((heads, members)),
            dma((tiles,)),
            dma((2, members)),
        ],
        compiler_params=pltpu.CompilerParams(
            collective_id=0, has_side_effects=True, vmem_limit_bytes=48 * 1024 * 1024
        ),
    )(frame_rank, frame_depth, tile_lists, past, qkv)


def body(qkv_now, past_cache, frame_rank, frame_depth, tile_lists):
    past = jnp.transpose(past_cache[0], (1, 0, 2))
    qkv = jnp.transpose(qkv_now, (1, 0, 2))
    call = call_by_tile if qkv.shape[0] % 2 else call_by_head
    return call(qkv, past, frame_rank, frame_depth, tile_lists)


def solution(mesh):
    in_specs = (P("space", "frame", None), P("frame", "space", None, None), P(), P(), P())
    out_specs = P("space", "frame")
    return jax.shard_map(body, mesh=mesh, in_specs=in_specs, out_specs=out_specs, check_vma=False)
```

```python
import functools
import math

import jax
import jax.numpy as jnp
from jax import lax
from jax.experimental import pallas as pl
from jax.experimental.pallas import tpu as pltpu
from jax.sharding import PartitionSpec as P

HIDDEN = -1e30
FLOOR = -1e29
MESH = pl.DeviceIdType.MESH
LOG2E = math.log2(math.e)


def attend_by_tile(
    frames,
    members,
    heads,
    rank_ref,
    depth_ref,
    lists_ref,
    past_ref,
    qkv_ref,
    out_ref,
    kv,
    queries,
    bias,
    lse_cols,
    share_out,
    share_in,
    lse_out,
    lse_in,
    local_sem,
    past_send,
    past_recv,
    fwd_send,
    fwd_recv,
    query_send,
    query_recv,
    share_send,
    share_recv,
    lse_send,
    lse_recv,
):
    toks = past_ref.shape[1]
    dim = past_ref.shape[2] // 2
    scale = LOG2E / math.sqrt(dim)
    fi = lax.axis_index("frame")
    si = lax.axis_index("space")
    group = si // 2
    core = si % 2
    beside = group * 2 + 1 - core
    peer = (fi, beside)
    size = members // 2
    half = group // size
    place = group - half * size
    passes = jnp.logical_or(group == 1, group == members - 2)
    end_from = jnp.where(group == 1, members - 1, 0)
    end_to = members - 1 - end_from

    def frame_at(slot):
        return lax.rem(fi + slot, frames)

    def device_of(member):
        return (fi, member * 2 + core)

    def remote(src, dst, send_sem, recv_sem, device):
        return pltpu.make_async_remote_copy(
            src_ref=src,
            dst_ref=dst,
            send_sem=send_sem,
            recv_sem=recv_sem,
            device_id=device,
            device_id_type=MESH,
        )

    def own_past(h):
        return past_ref.at[fi * heads + h]

    def own_now(h):
        return qkv_ref.at[h, :, pl.ds(dim, 2 * dim)]

    def own_query(h):
        return qkv_ref.at[h, :, pl.ds(0, dim)]

    def local_copies(h):
        return [
            pltpu.make_async_copy(own_past(h), kv.at[0, h, 0], local_sem.at[h, 0]),
            pltpu.make_async_copy(own_now(h), kv.at[0, h, frames], local_sem.at[h, 1]),
            pltpu.make_async_copy(own_query(h), queries.at[h, group], local_sem.at[h, 2]),
        ]

    def each(count, step):
        lax.fori_loop(0, count, lambda at, carry: (step(at), carry)[1], 0)

    def past_copy(h, j):
        to = frame_at(frames - j)
        return remote(
            past_ref.at[to * heads + h],
            kv.at[0, h, j],
            past_send.at[h, j],
            past_recv.at[h, j],
            (to, si),
        )

    def forward(h, j):
        src = kv.at[0, h, j]
        if j == 0:
            src = own_past(h)
        elif j == frames:
            src = own_now(h)
        return remote(src, kv.at[1, h, j], fwd_send.at[h, j], fwd_recv.at[h, j], peer)

    def query_copy(h, j):
        to = lax.rem(group + j, members)
        return jnp.abs(to - group) != members - 1, remote(
            own_query(h),
            queries.at[h, group],
            query_send.at[h, j],
            query_recv.at[h, group],
            device_of(to),
        )

    def query_on(h):
        return remote(
            queries.at[h, end_from],
            queries.at[h, end_from],
            query_send.at[h, 0],
            query_recv.at[h, end_from],
            device_of(end_to),
        )

    def query_wait(h, member):
        remote(
            queries.at[h, member],
            queries.at[h, member],
            query_send.at[h, 0],
            query_recv.at[h, member],
            peer,
        ).wait_recv()

    def start_past(h):
        for j in range(1, frames):
            past_copy(h, j).start()

    def start_query(h):
        for j in range(1, members):
            wanted, copy = query_copy(h, j)
            pl.when(wanted)(copy.start)

    barrier = pltpu.get_barrier_semaphore()
    partners = [(frame_at(j), si) for j in range(1, frames)]
    partners += [device_of(lax.rem(group + j, members)) for j in range(1, members)]
    partners.append(peer)
    for partner in partners:
        pl.semaphore_signal(barrier, inc=1, device_id=partner, device_id_type=MESH)
    pl.semaphore_wait(barrier, len(partners))

    def start_head(h):
        start_past(h)
        start_query(h)
        for j in (0, frames):
            forward(h, j).start()
        for copy in local_copies(h):
            copy.start()

    each(heads, start_head)
    lse_cols[...] = jnp.zeros_like(lse_cols)
    lanes = lax.broadcasted_iota(jnp.int32, (1, toks), 1)

    def bias_of(key_tile, slot, tile):
        sees = lists_ref[tile, key_tile] > 0
        if slot < frames:
            sees = jnp.logical_and(
                sees, rank_ref[frame_at(slot)] >= frames - depth_ref[tile]
            )
        return jnp.where(sees, 0.0, HIDDEN)

    blocks = [(side, slot) for side in range(2) for slot in range(frames + 1)]

    def set_bias(member):
        for at, (side, slot) in enumerate(blocks):
            bias[member, at] = bias_of((si, beside)[side], slot, member * 2 + core)

    each(members, set_bias)

    def share_copy(h, member):
        return remote(
            share_out.at[h, member],
            share_in.at[h, group],
            share_send.at[h, member],
            share_recv.at[h, group],
            device_of(member),
        )

    def unit(h, pair):
        query = queries[h, pl.ds(2 * pair, 2)].reshape(2 * toks, dim)
        keys = kv[:, h, :, :, :dim].reshape(len(blocks) * toks, dim)
        values = kv[:, h, :, :, dim:].reshape(len(blocks) * toks, dim)
        score = lax.dot_general(
            query, keys, (((1,), (1,)), ((), ())), preferred_element_type=jnp.float32
        )
        weights = []
        safes = []
        for at in range(2):
            member = 2 * pair + at
            rows = score[at * toks : (at + 1) * toks]
            parts = [
                rows[:, b * toks : (b + 1) * toks] + bias[member, b] for b in range(len(blocks))
            ]
            peak = jnp.max(functools.reduce(jnp.maximum, parts), axis=1, keepdims=True)
            peak = jnp.maximum(peak, FLOOR) * scale
            parts = [jnp.exp2(part * scale - peak) for part in parts]
            total = jnp.sum(functools.reduce(jnp.add, parts), axis=1, keepdims=True)
            safe = jnp.maximum(total, 1.0)
            safes.append(safe)
            lse = peak + jnp.log(safe) * LOG2E
            lse_cols[member] = jnp.where(lanes == h, lse, lse_cols[member])
            weights.append(jnp.concatenate([part.astype(jnp.bfloat16) for part in parts], 1))
        weighted = jnp.dot(
            jnp.concatenate(weights, 0), values, preferred_element_type=jnp.float32
        )
        for at in range(2):
            member = 2 * pair + at
            share = weighted[at * toks : (at + 1) * toks] * (1.0 / safes[at])
            share_out[h, member] = share.astype(jnp.bfloat16)
            pl.when(member != group)(share_copy(h, member).start)

    def pass_on(h):
        for j in range(1, frames):
            past_copy(h, j).wait_recv()
            forward(h, j).start()

    def head(h):
        for copy in local_copies(h):
            copy.wait()
        for j in range(frames + 1):
            forward(h, j).wait_recv()

        def step(k):
            pair = lax.rem((1 - half) * (size // 2) + k, size)
            for at in range(2):
                member = 2 * pair + at
                pl.when(member != group)(functools.partial(query_wait, h, member))

                @pl.when(jnp.logical_and(passes, member == end_from))
                def _():
                    query_on(h).start()

            unit(h, pair)

            @pl.when(jnp.logical_and(k == 0, h + 1 < heads))
            def _():
                pass_on(h + 1)

        each(size, step)

    pass_on(0)
    each(heads, head)

    for member in range(members):
        lse_out[member] = lse_cols[member].T[: lse_out.shape[1]]

    def lse_copy(j):
        member = lax.rem(group + j, members)
        return remote(
            lse_out.at[member],
            lse_in.at[group],
            lse_send.at[member],
            lse_recv.at[group],
            device_of(member),
        )

    for j in range(1, members):
        lse_copy(j).start()

    def arrived(j):
        member = lax.rem(group + j, members)
        return member, remote(
            lse_out.at[member], lse_in.at[member], lse_send.at[member], lse_recv.at[member], peer
        )

    for j in range(1, members):
        arrived(j)[1].wait_recv()
    rows = [lse_out[group]]
    for j in range(1, members):
        rows.append(lse_in[lax.rem(group + j, members)])
    top = functools.reduce(jnp.maximum, rows)
    factors = [jnp.exp2(row - top) for row in rows]
    inverse = 1.0 / functools.reduce(jnp.add, factors)
    columns = [(factor * inverse).T for factor in factors]
    for h in range(heads):
        summed = share_out[h, group].astype(jnp.float32) * columns[0][:, h : h + 1]
        for j in range(1, members):
            member = lax.rem(group + j, members)
            remote(
                share_out.at[h, member],
                share_in.at[h, member],
                share_send.at[h, member],
                share_recv.at[h, member],
                peer,
            ).wait_recv()
            summed += share_in[h, member].astype(jnp.float32) * columns[j][:, h : h + 1]
        out_ref[:, h * dim : (h + 1) * dim] = summed.astype(out_ref.dtype)

    def sent(h):
        for j in range(1, frames):
            past_copy(h, j).wait_send()
        for j in range(frames + 1):
            forward(h, j).wait_send()
        for j in range(1, members):
            wanted, copy = query_copy(h, j)
            pl.when(wanted)(copy.wait_send)
            share_copy(h, lax.rem(group + j, members)).wait_send()
        pl.when(passes)(query_on(h).wait_send)

    each(heads, sent)
    for j in range(1, members):
        lse_copy(j).wait_send()


def call_by_tile(qkv, past, frame_rank, frame_depth, tile_lists):
    heads, toks, width = qkv.shape
    dim = width // 3
    frames = lax.axis_size("frame")
    members = lax.axis_size("space") // 2
    lse_rows = -(-heads // 8) * 8
    dma = pltpu.SemaphoreType.DMA
    smem = pl.BlockSpec(memory_space=pltpu.SMEM)
    return pl.pallas_call(
        functools.partial(attend_by_tile, frames, members, heads),
        out_shape=jax.ShapeDtypeStruct((toks, heads * dim), jnp.bfloat16),
        in_specs=[smem, smem, smem] + [pl.BlockSpec(memory_space=pl.ANY)] * 2,
        out_specs=pl.BlockSpec(memory_space=pltpu.VMEM),
        scratch_shapes=[
            pltpu.VMEM((2, heads, frames + 1, toks, 2 * dim), jnp.bfloat16),
            pltpu.VMEM((heads, members, toks, dim), jnp.bfloat16),
            pltpu.SMEM((members, 2 * (frames + 1)), jnp.float32),
            pltpu.VMEM((members, toks, toks), jnp.float32),
            pltpu.VMEM((heads, members, toks, dim), jnp.bfloat16),
            pltpu.VMEM((heads, members, toks, dim), jnp.bfloat16),
            pltpu.VMEM((members, lse_rows, toks), jnp.float32),
            pltpu.VMEM((members, lse_rows, toks), jnp.float32),
            dma((heads, 3)),
            dma((heads, frames)),
            dma((heads, frames)),
            dma((heads, frames + 1)),
            dma((heads, frames + 1)),
            dma((heads, members)),
            dma((heads, members)),
            dma((heads, members)),
            dma((heads, members)),
            dma((members,)),
            dma((members,)),
        ],
        compiler_params=pltpu.CompilerParams(
            collective_id=0, has_side_effects=True, vmem_limit_bytes=48 * 1024 * 1024
        ),
    )(frame_rank, frame_depth, tile_lists, past, qkv)


def attend_by_head(
    frames,
    members,
    heads,
    rank_ref,
    depth_ref,
    lists_ref,
    past_ref,
    qkv_ref,
    out_ref,
    kv,
    queries,
    bias,
    lse_cols,
    share_out,
    share_in,
    lse_out,
    lse_in,
    local_sem,
    past_send,
    past_recv,
    query_send,
    query_recv,
    share_send,
    share_recv,
    lse_send,
    lse_recv,
):
    toks = past_ref.shape[1]
    dim = past_ref.shape[2] // 2
    own = heads // 2
    tiles = 2 * members
    scale = LOG2E / math.sqrt(dim)
    fi = lax.axis_index("frame")
    si = lax.axis_index("space")
    group = si // 2
    core = si % 2
    peer = (fi, group * 2 + 1 - core)
    half = group // (members // 2)

    def frame_at(slot):
        return lax.rem(fi + slot, frames)

    def core_at(e):
        return core if e == 0 else 1 - core

    def tile_at(j):
        return lax.rem(si + j, tiles)

    def remote(src, dst, send_sem, recv_sem, device):
        return pltpu.make_async_remote_copy(
            src_ref=src,
            dst_ref=dst,
            send_sem=send_sem,
            recv_sem=recv_sem,
            device_id=device,
            device_id_type=MESH,
        )

    def each(count, step):
        lax.fori_loop(0, count, lambda at, carry: (step(at), carry)[1], 0)

    def past_source(e, j):
        to = fi if j in (0, frames) else frame_at(frames - j)
        if j == frames:
            return to, qkv_ref.at[pl.ds(core_at(e) * own, own), :, pl.ds(dim, 2 * dim)]
        return to, past_ref.at[pl.ds(to * heads + core_at(e) * own, own)]

    def query_source(to_core):
        return qkv_ref.at[pl.ds(to_core * own, own), :, pl.ds(0, dim)]

    local = [
        pltpu.make_async_copy(past_source(0, 0)[1], kv.at[core, 0], local_sem.at[0]),
        pltpu.make_async_copy(past_source(0, frames)[1], kv.at[core, frames], local_sem.at[1]),
        pltpu.make_async_copy(query_source(core), queries.at[si], local_sem.at[2]),
    ]

    sent_blocks = [(e, j) for j in range(1, frames) for e in range(2)] + [(1, 0), (1, frames)]

    def past_copy(e, j):
        to, src = past_source(e, j)
        return remote(
            src,
            kv.at[core, j],
            past_send.at[e, j],
            past_recv.at[core, j],
            (to, group * 2 + core_at(e)),
        )

    def past_wait(e, j):
        block = kv.at[core_at(e), j]
        remote(block, block, past_send.at[e, j], past_recv.at[core_at(e), j], peer).wait_recv()

    def query_copy(j):
        to = tile_at(j)
        return remote(
            query_source(lax.rem(to, 2)),
            queries.at[si],
            query_send.at[j],
            query_recv.at[si],
            (fi, to),
        )

    def query_wait(tile):
        block = queries.at[tile]
        remote(block, block, query_send.at[0], query_recv.at[tile], peer).wait_recv()

    barrier = pltpu.get_barrier_semaphore()
    partners = [(frame_at(j), group * 2 + e) for j in range(1, frames) for e in range(2)]
    partners += [(fi, tile_at(j)) for j in range(1, tiles)]
    for partner in partners:
        pl.semaphore_signal(barrier, inc=1, device_id=partner, device_id_type=MESH)
    pl.semaphore_wait(barrier, len(partners))

    for e, j in sent_blocks:
        past_copy(e, j).start()
    for j in range(1, tiles):
        query_copy(j).start()
    for copy in local:
        copy.start()

    lse_cols[...] = jnp.zeros_like(lse_cols)
    lanes = lax.broadcasted_iota(jnp.int32, (1, toks), 1)

    def bias_of(key_tile, slot, tile):
        sees = lists_ref[tile, key_tile] > 0
        if slot < frames:
            sees = jnp.logical_and(
                sees, rank_ref[frame_at(slot)] >= frames - depth_ref[tile]
            )
        return jnp.where(sees, 0.0, HIDDEN)

    blocks = [(side, slot) for side in range(2) for slot in range(frames + 1)]

    def set_bias(tile):
        for at, (side, slot) in enumerate(blocks):
            bias[tile, at] = bias_of(group * 2 + side, slot, tile)

    each(tiles, set_bias)

    def share_copy(tile):
        return remote(
            share_out.at[tile],
            share_in.at[core, group],
            share_send.at[tile],
            share_recv.at[core, group],
            (fi, tile),
        )

    def unit(h, member):
        query = queries[pl.ds(2 * member, 2), h].reshape(2 * toks, dim)
        keys = kv[:, :, h, :, :dim].reshape(len(blocks) * toks, dim)
        values = kv[:, :, h, :, dim:].reshape(len(blocks) * toks, dim)
        score = lax.dot_general(
            query, keys, (((1,), (1,)), ((), ())), preferred_element_type=jnp.float32
        )
        weights = []
        safes = []
        for at in range(2):
            tile = 2 * member + at
            rows = score[at * toks : (at + 1) * toks]
            parts = [
                rows[:, b * toks : (b + 1) * toks] + bias[tile, b] for b in range(len(blocks))
            ]
            peak = jnp.max(functools.reduce(jnp.maximum, parts), axis=1, keepdims=True)
            peak = jnp.maximum(peak, FLOOR) * scale
            parts = [jnp.exp2(part * scale - peak) for part in parts]
            total = jnp.sum(functools.reduce(jnp.add, parts), axis=1, keepdims=True)
            safe = jnp.maximum(total, 1.0)
            safes.append(safe)
            lse = peak + jnp.log(safe) * LOG2E
            lse_cols[tile] = jnp.where(lanes == h, lse, lse_cols[tile])
            weights.append(jnp.concatenate([part.astype(jnp.bfloat16) for part in parts], 1))
        weighted = jnp.dot(
            jnp.concatenate(weights, 0), values, preferred_element_type=jnp.float32
        )
        for at in range(2):
            tile = 2 * member + at
            share = weighted[at * toks : (at + 1) * toks] * (1.0 / safes[at])
            share_out[tile, h] = share.astype(jnp.bfloat16)

    for copy in local:
        copy.wait()
    for e, j in sent_blocks:
        past_wait(e, j)

    def step(k):
        member = lax.rem((1 - half) * (members // 2) + k, members)
        for at in range(2):
            tile = 2 * member + at
            pl.when(tile != si)(functools.partial(query_wait, tile))
        each(own, lambda h: unit(h, member))
        for at in range(2):
            tile = 2 * member + at
            pl.when(tile != si)(share_copy(tile).start)

    each(members, step)

    for tile in range(tiles):
        lse_out[tile] = lse_cols[tile].T[: lse_out.shape[1]]

    def lse_copy(j):
        tile = tile_at(j)
        return remote(
            lse_out.at[tile],
            lse_in.at[core, group],
            lse_send.at[tile],
            lse_recv.at[core, group],
            (fi, tile),
        )

    for j in range(1, tiles):
        lse_copy(j).start()
    lse_in[core, group] = lse_out[si]
    share_in[core, group] = share_out[si]
    for j in range(1, tiles):
        tile = tile_at(j)
        block = lse_in.at[lax.rem(tile, 2), tile // 2]
        remote(
            block, block, lse_send.at[tile], lse_recv.at[lax.rem(tile, 2), tile // 2], peer
        ).wait_recv()
    for c in range(2):
        rows = [lse_in[c, m] for m in range(members)]
        top = functools.reduce(jnp.maximum, rows)
        factors = [jnp.exp2(row - top) for row in rows]
        inverse = 1.0 / functools.reduce(jnp.add, factors)
        columns = [(factor * inverse).T for factor in factors]
        for m in range(members):
            block = share_in.at[c, m]
            pl.when(2 * m + c != si)(
                remote(block, block, share_send.at[0], share_recv.at[c, m], peer).wait_recv
            )
        for h in range(own):
            at = c * own + h
            summed = 0.0
            for m in range(members):
                summed += share_in[c, m, h].astype(jnp.float32) * columns[m][:, h : h + 1]
            out_ref[:, at * dim : (at + 1) * dim] = summed.astype(out_ref.dtype)

    for e, j in sent_blocks:
        past_copy(e, j).wait_send()
    for j in range(1, tiles):
        query_copy(j).wait_send()
        share_copy(tile_at(j)).wait_send()
        lse_copy(j).wait_send()


def call_by_head(qkv, past, frame_rank, frame_depth, tile_lists):
    heads, toks, width = qkv.shape
    dim = width // 3
    frames = lax.axis_size("frame")
    tiles = lax.axis_size("space")
    members = tiles // 2
    own = heads // 2
    lse_rows = -(-own // 8) * 8
    dma = pltpu.SemaphoreType.DMA
    smem = pl.BlockSpec(memory_space=pltpu.SMEM)
    return pl.pallas_call(
        functools.partial(attend_by_head, frames, members, heads),
        out_shape=jax.ShapeDtypeStruct((toks, heads * dim), jnp.bfloat16),
        in_specs=[smem, smem, smem] + [pl.BlockSpec(memory_space=pl.ANY)] * 2,
        out_specs=pl.BlockSpec(memory_space=pltpu.VMEM),
        scratch_shapes=[
            pltpu.VMEM((2, frames + 1, own, toks, 2 * dim), jnp.bfloat16),
            pltpu.VMEM((tiles, own, toks, dim), jnp.bfloat16),
            pltpu.SMEM((tiles, 2 * (frames + 1)), jnp.float32),
            pltpu.VMEM((tiles, toks, toks), jnp.float32),
            pltpu.VMEM((tiles, own, toks, dim), jnp.bfloat16),
            pltpu.VMEM((2, members, own, toks, dim), jnp.bfloat16),
            pltpu.VMEM((tiles, lse_rows, toks), jnp.float32),
            pltpu.VMEM((2, members, lse_rows, toks), jnp.float32),
            dma((3,)),
            dma((2, frames + 1)),
            dma((2, frames + 1)),
            dma((tiles,)),
            dma((tiles,)),
            dma((tiles,)),
            dma((2, members)),
            dma((tiles,)),
            dma((2, members)),
        ],
        compiler_params=pltpu.CompilerParams(
            collective_id=0, has_side_effects=True, vmem_limit_bytes=48 * 1024 * 1024
        ),
    )(frame_rank, frame_depth, tile_lists, past, qkv)


def body(qkv_now, past_cache, frame_rank, frame_depth, tile_lists):
    past = jnp.transpose(past_cache[0], (1, 0, 2))
    qkv = jnp.transpose(qkv_now, (1, 0, 2))
    call = call_by_tile if qkv.shape[0] % 2 else call_by_head
    return call(qkv, past, frame_rank, frame_depth, tile_lists)


def solution(mesh):
    in_specs = (P("space", "frame", None), P("frame", "space", None, None), P(), P(), P())
    out_specs = P("space", "frame")
    return jax.shard_map(body, mesh=mesh, in_specs=in_specs, out_specs=out_specs, check_vma=False)
```

```python
import functools
import math

import jax
import jax.numpy as jnp
from jax import lax
from jax.experimental import pallas as pl
from jax.experimental.pallas import tpu as pltpu
from jax.sharding import PartitionSpec as P

HIDDEN = -1e30
FLOOR = -1e29
MESH = pl.DeviceIdType.MESH
LOG2E = math.log2(math.e)


def attend(
    frames,
    members,
    heads,
    rank_ref,
    depth_ref,
    lists_ref,
    past_ref,
    qkv_ref,
    out_ref,
    kv,
    queries,
    bias,
    lse_cols,
    share_out,
    share_in,
    lse_out,
    lse_in,
    local_sem,
    past_send,
    past_recv,
    fwd_send,
    fwd_recv,
    query_send,
    query_recv,
    share_send,
    share_recv,
    lse_send,
    lse_recv,
):
    toks = past_ref.shape[1]
    dim = past_ref.shape[2] // 2
    scale = LOG2E / math.sqrt(dim)
    fi = lax.axis_index("frame")
    si = lax.axis_index("space")
    group = si // 2
    core = si % 2
    beside = group * 2 + 1 - core
    peer = (fi, beside)
    size = members // 2
    half = group // size

    def frame_at(slot):
        return lax.rem(fi + slot, frames)

    def device_of(member):
        return (fi, member * 2 + core)

    def remote(src, dst, send_sem, recv_sem, device):
        return pltpu.make_async_remote_copy(
            src_ref=src,
            dst_ref=dst,
            send_sem=send_sem,
            recv_sem=recv_sem,
            device_id=device,
            device_id_type=MESH,
        )

    def own_past(h):
        return past_ref.at[fi * heads + h]

    def own_now(h):
        return qkv_ref.at[h, :, pl.ds(dim, 2 * dim)]

    def own_query(h):
        return qkv_ref.at[h, :, pl.ds(0, dim)]

    def local_copies(h):
        return [
            pltpu.make_async_copy(own_past(h), kv.at[0, h, 0], local_sem.at[h, 0]),
            pltpu.make_async_copy(own_now(h), kv.at[0, h, frames], local_sem.at[h, 1]),
            pltpu.make_async_copy(own_query(h), queries.at[h, group], local_sem.at[h, 2]),
        ]

    def each(count, step):
        lax.fori_loop(0, count, lambda at, carry: (step(at), carry)[1], 0)

    def past_copy(h, j):
        to = frame_at(frames - j)
        return remote(
            past_ref.at[to * heads + h],
            kv.at[0, h, j],
            past_send.at[h, j],
            past_recv.at[h, j],
            (to, si),
        )

    def forward(h, j):
        src = kv.at[0, h, j]
        if j == 0:
            src = own_past(h)
        elif j == frames:
            src = own_now(h)
        return remote(src, kv.at[1, h, j], fwd_send.at[h, j], fwd_recv.at[h, j], peer)

    def query_copy(h, j):
        to = lax.rem(group + j, members)
        return remote(
            own_query(h),
            queries.at[h, group],
            query_send.at[h, j],
            query_recv.at[h, group],
            device_of(to),
        )

    def query_wait(h, member):
        remote(
            queries.at[h, member],
            queries.at[h, member],
            query_send.at[h, 0],
            query_recv.at[h, member],
            peer,
        ).wait_recv()

    def start_past(h):
        for j in range(1, frames):
            past_copy(h, j).start()

    def start_query(h):
        for j in range(1, members):
            query_copy(h, j).start()


    barrier = pltpu.get_barrier_semaphore()
    partners = [(frame_at(j), si) for j in range(1, frames)]
    partners += [device_of(lax.rem(group + j, members)) for j in range(1, members)]
    partners.append(peer)
    for partner in partners:
        pl.semaphore_signal(barrier, inc=1, device_id=partner, device_id_type=MESH)
    pl.semaphore_wait(barrier, len(partners))

    def start_head(h):
        start_past(h)
        start_query(h)
        for j in (0, frames):
            forward(h, j).start()
        for copy in local_copies(h):
            copy.start()

    each(heads, start_head)
    lse_cols[...] = jnp.zeros_like(lse_cols)
    lanes = lax.broadcasted_iota(jnp.int32, (1, toks), 1)

    def bias_of(key_tile, slot, tile):
        sees = lists_ref[tile, key_tile] > 0
        if slot < frames:
            sees = jnp.logical_and(
                sees, rank_ref[frame_at(slot)] >= frames - depth_ref[tile]
            )
        return jnp.where(sees, 0.0, HIDDEN)

    blocks = [(side, slot) for side in range(2) for slot in range(frames + 1)]

    def set_bias(member):
        for at, (side, slot) in enumerate(blocks):
            bias[member, at] = bias_of((si, beside)[side], slot, member * 2 + core)

    each(members, set_bias)

    def share_copy(h, member):
        return remote(
            share_out.at[h, member],
            share_in.at[h, group],
            share_send.at[h, member],
            share_recv.at[h, group],
            device_of(member),
        )

    def unit(h, pair):
        query = queries[h, pl.ds(2 * pair, 2)].reshape(2 * toks, dim)
        keys = kv[:, h, :, :, :dim].reshape(len(blocks) * toks, dim)
        values = kv[:, h, :, :, dim:].reshape(len(blocks) * toks, dim)
        score = lax.dot_general(
            query, keys, (((1,), (1,)), ((), ())), preferred_element_type=jnp.float32
        )
        weights = []
        safes = []
        for at in range(2):
            member = 2 * pair + at
            rows = score[at * toks : (at + 1) * toks]
            parts = [
                rows[:, b * toks : (b + 1) * toks] + bias[member, b] for b in range(len(blocks))
            ]
            peak = jnp.max(functools.reduce(jnp.maximum, parts), axis=1, keepdims=True)
            peak = jnp.maximum(peak, FLOOR) * scale
            parts = [jnp.exp2(part * scale - peak) for part in parts]
            total = jnp.sum(functools.reduce(jnp.add, parts), axis=1, keepdims=True)
            safe = jnp.maximum(total, 1.0)
            safes.append(safe)
            lse = peak + jnp.log(safe) * LOG2E
            lse_cols[member] = jnp.where(lanes == h, lse, lse_cols[member])
            weights.append(jnp.concatenate([part.astype(jnp.bfloat16) for part in parts], 1))
        weighted = jnp.dot(
            jnp.concatenate(weights, 0), values, preferred_element_type=jnp.float32
        )
        for at in range(2):
            member = 2 * pair + at
            share = weighted[at * toks : (at + 1) * toks] * (1.0 / safes[at])
            share_out[h, member] = share.astype(jnp.bfloat16)
            pl.when(member != group)(share_copy(h, member).start)

    def pass_on(h):
        for j in range(1, frames):
            past_copy(h, j).wait_recv()
            forward(h, j).start()

    def head(h):
        for copy in local_copies(h):
            copy.wait()
        for j in range(frames + 1):
            forward(h, j).wait_recv()

        def step(k):
            pair = lax.rem((1 - half) * (size // 2) + k, size)
            for at in range(2):
                member = 2 * pair + at
                pl.when(member != group)(functools.partial(query_wait, h, member))

            unit(h, pair)

            if k == 0 and h + 1 < heads:
                pass_on(h + 1)

        for k in range(size):
            step(k)

    pass_on(0)
    for h in range(heads):
        head(h)

    for member in range(members):
        lse_out[member] = lse_cols[member].T[: lse_out.shape[1]]

    def lse_copy(j):
        member = lax.rem(group + j, members)
        return remote(
            lse_out.at[member],
            lse_in.at[group],
            lse_send.at[member],
            lse_recv.at[group],
            device_of(member),
        )

    for j in range(1, members):
        lse_copy(j).start()

    def arrived(j):
        member = lax.rem(group + j, members)
        return member, remote(
            lse_out.at[member], lse_in.at[member], lse_send.at[member], lse_recv.at[member], peer
        )

    for j in range(1, members):
        arrived(j)[1].wait_recv()
    rows = [lse_out[group]]
    for j in range(1, members):
        rows.append(lse_in[lax.rem(group + j, members)])
    top = functools.reduce(jnp.maximum, rows)
    factors = [jnp.exp2(row - top) for row in rows]
    inverse = 1.0 / functools.reduce(jnp.add, factors)
    columns = [(factor * inverse).T for factor in factors]
    for h in range(heads):
        summed = share_out[h, group].astype(jnp.float32) * columns[0][:, h : h + 1]
        for j in range(1, members):
            member = lax.rem(group + j, members)
            remote(
                share_out.at[h, member],
                share_in.at[h, member],
                share_send.at[h, member],
                share_recv.at[h, member],
                peer,
            ).wait_recv()
            summed += share_in[h, member].astype(jnp.float32) * columns[j][:, h : h + 1]
        out_ref[:, h * dim : (h + 1) * dim] = summed.astype(out_ref.dtype)

    def sent(h):
        for j in range(1, frames):
            past_copy(h, j).wait_send()
        for j in range(frames + 1):
            forward(h, j).wait_send()
        for j in range(1, members):
            query_copy(h, j).wait_send()
            share_copy(h, lax.rem(group + j, members)).wait_send()

    each(heads, sent)
    for j in range(1, members):
        lse_copy(j).wait_send()


def body(qkv_now, past_cache, frame_rank, frame_depth, tile_lists):
    toks, heads, width = qkv_now.shape
    dim = width // 3
    frames = lax.axis_size("frame")
    members = lax.axis_size("space") // 2
    past = jnp.transpose(past_cache[0], (1, 0, 2))
    qkv = jnp.transpose(qkv_now, (1, 0, 2))
    lse_rows = -(-heads // 8) * 8
    dma = pltpu.SemaphoreType.DMA
    smem = pl.BlockSpec(memory_space=pltpu.SMEM)
    return pl.pallas_call(
        functools.partial(attend, frames, members, heads),
        out_shape=jax.ShapeDtypeStruct((toks, heads * dim), jnp.bfloat16),
        in_specs=[smem, smem, smem] + [pl.BlockSpec(memory_space=pl.ANY)] * 2,
        out_specs=pl.BlockSpec(memory_space=pltpu.VMEM),
        scratch_shapes=[
            pltpu.VMEM((2, heads, frames + 1, toks, 2 * dim), jnp.bfloat16),
            pltpu.VMEM((heads, members, toks, dim), jnp.bfloat16),
            pltpu.SMEM((members, 2 * (frames + 1)), jnp.float32),
            pltpu.VMEM((members, toks, toks), jnp.float32),
            pltpu.VMEM((heads, members, toks, dim), jnp.bfloat16),
            pltpu.VMEM((heads, members, toks, dim), jnp.bfloat16),
            pltpu.VMEM((members, lse_rows, toks), jnp.float32),
            pltpu.VMEM((members, lse_rows, toks), jnp.float32),
            dma((heads, 3)),
            dma((heads, frames)),
            dma((heads, frames)),
            dma((heads, frames + 1)),
            dma((heads, frames + 1)),
            dma((heads, members)),
            dma((heads, members)),
            dma((heads, members)),
            dma((heads, members)),
            dma((members,)),
            dma((members,)),
        ],
        compiler_params=pltpu.CompilerParams(
            collective_id=0, has_side_effects=True, vmem_limit_bytes=48 * 1024 * 1024
        ),
    )(frame_rank, frame_depth, tile_lists, past, qkv)


def solution(mesh):
    in_specs = (P("space", "frame", None), P("frame", "space", None, None), P(), P(), P())
    out_specs = P("space", "frame")
    return jax.shard_map(body, mesh=mesh, in_specs=in_specs, out_specs=out_specs, check_vma=False)
```

```python
import functools
import math

import jax
import jax.numpy as jnp
from jax import lax
from jax.experimental import pallas as pl
from jax.experimental.pallas import tpu as pltpu
from jax.sharding import PartitionSpec as P

HIDDEN = -1e30
FLOOR = -1e29
MESH = pl.DeviceIdType.MESH
LOG2E = math.log2(math.e)


def attend(
    frames,
    members,
    heads,
    rank_ref,
    depth_ref,
    lists_ref,
    past_ref,
    qkv_ref,
    out_ref,
    early_kv,
    late_kv,
    queries,
    early_values,
    late_values,
    bias_rows,
    part_sum,
    part_stat,
    share_out,
    share_in,
    lse_out,
    lse_in,
    local_sem,
    past_send,
    past_recv,
    fwd_send,
    fwd_recv,
    query_send,
    query_recv,
    share_send,
    share_recv,
    lse_send,
    lse_recv,
):
    toks = past_ref.shape[1]
    dim = past_ref.shape[2] // 2
    scale = LOG2E / math.sqrt(dim)
    fi = lax.axis_index("frame")
    si = lax.axis_index("space")
    group = si // 2
    core = si % 2
    beside = group * 2 + 1 - core
    peer = (fi, beside)
    size = members // 2
    half = group // size
    place = group - half * size

    def frame_at(slot):
        return lax.rem(fi + slot, frames)

    def device_of(member):
        return (fi, member * 2 + core)

    def remote(src, dst, send_sem, recv_sem, device):
        return pltpu.make_async_remote_copy(
            src_ref=src,
            dst_ref=dst,
            send_sem=send_sem,
            recv_sem=recv_sem,
            device_id=device,
            device_id_type=MESH,
        )

    def own_past(h):
        return past_ref.at[fi * heads + h]

    def own_now(h):
        return qkv_ref.at[h, :, pl.ds(dim, 2 * dim)]

    def own_query(h):
        return qkv_ref.at[h, :, pl.ds(0, dim)]

    local = [
        [
            pltpu.make_async_copy(own_past(h), early_kv.at[0, h, 0], local_sem.at[h, 0]),
            pltpu.make_async_copy(own_now(h), early_kv.at[0, h, 1], local_sem.at[h, 1]),
            pltpu.make_async_copy(own_query(h), queries.at[h, group], local_sem.at[h, 2]),
        ]
        for h in range(heads)
    ]
    for copies in local:
        for copy in copies:
            copy.start()

    def past_copy(h, j):
        to = frame_at(frames - j)
        return remote(
            past_ref.at[to * heads + h],
            late_kv.at[0, h, j - 1],
            past_send.at[h, j],
            past_recv.at[h, j],
            (to, si),
        )

    def early_forward(h, j):
        return remote(
            (own_past, own_now)[j](h),
            early_kv.at[1, h, j],
            fwd_send.at[h, frames - 1 + j],
            fwd_recv.at[h, frames - 1 + j],
            peer,
        )

    def late_forward(h, j):
        return remote(
            late_kv.at[0, h, j],
            late_kv.at[1, h, j],
            fwd_send.at[h, j],
            fwd_recv.at[h, j],
            peer,
        )

    def query_copy(h, j):
        to = lax.rem(group + j, members)
        return remote(
            own_query(h),
            queries.at[h, group],
            query_send.at[h, j],
            query_recv.at[h, group],
            device_of(to),
        )

    def query_wait(h, member):
        remote(
            queries.at[h, member],
            queries.at[h, member],
            query_send.at[h, 0],
            query_recv.at[h, member],
            peer,
        ).wait_recv()

    def start_past(h):
        for j in range(1, frames):
            past_copy(h, j).start()

    def start_query(h):
        for j in range(1, members):
            query_copy(h, j).start()

    barrier = pltpu.get_barrier_semaphore()
    partners = [(frame_at(j), si) for j in range(1, frames)]
    partners += [device_of(lax.rem(group + j, members)) for j in range(1, members)]
    partners.append(peer)
    for partner in partners:
        pl.semaphore_signal(barrier, inc=1, device_id=partner, device_id_type=MESH)
    pl.semaphore_wait(barrier, len(partners))

    ahead = heads
    for h in range(ahead):
        start_past(h)
        start_query(h)
        for j in range(2):
            early_forward(h, j).start()
    for h in range(ahead, heads):
        for j in range(2):
            early_forward(h, j).start()

    lse_out[...] = jnp.zeros_like(lse_out)
    lanes = lax.broadcasted_iota(jnp.int32, (1, 2 * toks), 1)

    def bias_of(key_tile, slot, tile):
        sees = lists_ref[tile, key_tile] > 0
        if slot < frames:
            sees = jnp.logical_and(
                sees, rank_ref[frame_at(slot)] >= frames - depth_ref[tile]
            )
        return jnp.where(sees, 0.0, HIDDEN)

    late_slots = frames - 1
    blocks = [(side, slot) for side in range(2) for slot in (0, frames)]
    blocks += [(side, slot) for side in range(2) for slot in range(1, frames)]
    early_count = 4
    for pair in range(size):
        for at, (side, slot) in enumerate(blocks):
            low, high = (
                bias_of((si, beside)[side], slot, (2 * pair + k) * 2 + core) for k in range(2)
            )
            bias_rows[pair, at : at + 1, :] = jnp.where(lanes < toks, low, high)

    def weigh(keys, query, pair, first, count, peak):
        score = lax.dot_general(
            keys, query, (((1,), (1,)), ((), ())), preferred_element_type=jnp.float32
        )
        parts = [score[at * toks : (at + 1) * toks] for at in range(count)]
        bias = [bias_rows[pair, first + at : first + at + 1, :] for at in range(count)]
        for part, row in zip(parts, bias):
            peak = jnp.maximum(peak, jnp.max(part, axis=0, keepdims=True) * scale + row)
        total = jnp.zeros((1, 2 * toks), jnp.float32)
        weights = []
        for part, row in zip(parts, bias):
            weight = jnp.exp2(part * scale - (peak - row))
            total += jnp.sum(weight, axis=0, keepdims=True)
            weights.append(weight.astype(jnp.bfloat16))
        return peak, total, jnp.concatenate(weights, 0)

    def query_of(h, pair):
        return queries[h, pl.ds(2 * pair, 2)].reshape(2 * toks, dim)

    def early(h, pair):
        keys = early_kv[:, h, :, :, :dim].reshape(4 * toks, dim)
        floor = jnp.full((1, 2 * toks), FLOOR, jnp.float32)
        peak, total, weights = weigh(keys, query_of(h, pair), pair, 0, early_count, floor)
        part_sum[h, pair] = jnp.dot(early_values[...], weights, preferred_element_type=jnp.float32)
        part_stat[h, pair, 0:1, :] = peak
        part_stat[h, pair, 1:2, :] = total

    def share_copy(h, member):
        return remote(
            share_out.at[h, member],
            share_in.at[h, group],
            share_send.at[h, member],
            share_recv.at[h, group],
            device_of(member),
        )

    def late(h, pair):
        keys = late_kv[:, h, :, :, :dim].reshape(2 * late_slots * toks, dim)
        before = part_stat[h, pair, 0:1, :]
        peak, total, weights = weigh(
            keys, query_of(h, pair), pair, early_count, 2 * late_slots, before
        )
        factor = jnp.exp2(before - peak)
        safe = jnp.maximum(total + part_stat[h, pair, 1:2, :] * factor, 1.0)
        inverse = 1.0 / safe
        weighted = jnp.dot(late_values[...], weights, preferred_element_type=jnp.float32)
        share = (weighted * inverse + part_sum[h, pair] * (factor * inverse)).astype(jnp.bfloat16)
        lse = peak + jnp.log(safe) * LOG2E
        for at in range(2):
            member = 2 * pair + at
            share_out[h, member] = share[:, at * toks : (at + 1) * toks]
            lse_out[member, h : h + 1, :] = lse[:, at * toks : (at + 1) * toks]
            pl.when(member != group)(share_copy(h, member).start)

    def early_head(h):
        for copy in local[h]:
            copy.wait()
        for j in range(2):
            early_forward(h, j).wait_recv()
        for side in range(2):
            for j in range(2):
                at = (2 * side + j) * toks
                early_values[:, at : at + toks] = early_kv[side, h, j, :, dim:].T
        for d in range(1, size):
            query_wait(h, half * size + lax.rem(place + d, size))
        for k in range(size // 2):
            early(h, half * (size // 2) + k)

        for i in range(size):
            member = (1 - half) * size + i
            query_wait(h, member)
        if h + ahead < heads:
            start_query(h + ahead)
        for k in range(size // 2):
            early(h, (1 - half) * (size // 2) + k)

    def pass_on(h):
        for j in range(1, frames):
            past_copy(h, j).wait_recv()
            late_forward(h, j - 1).start()
        if h + ahead < heads:
            start_past(h + ahead)

    def late_head(h):
        for j in range(late_slots):
            late_forward(h, j).wait_recv()
        for side in range(2):
            for j in range(late_slots):
                at = (side * late_slots + j) * toks
                late_values[:, at : at + toks] = late_kv[side, h, j, :, dim:].T
        for part in (1 - half, half):
            for k in range(size // 2):
                late(h, part * (size // 2) + k)

    passed = 0
    for h in range(heads):
        early_head(h)
        if 1 <= h <= heads - 2:
            pass_on(passed)
            passed += 1
    for h in range(heads):
        while passed <= h:
            pass_on(passed)
            passed += 1
        late_head(h)
        if passed < heads:
            pass_on(passed)
            passed += 1

    def lse_copy(j):
        member = lax.rem(group + j, members)
        return remote(
            lse_out.at[member],
            lse_in.at[group],
            lse_send.at[member],
            lse_recv.at[group],
            device_of(member),
        )

    for j in range(1, members):
        lse_copy(j).start()

    def arrived(j):
        member = lax.rem(group + j, members)
        return member, remote(
            lse_out.at[member], lse_in.at[member], lse_send.at[member], lse_recv.at[member], peer
        )

    for j in range(1, members):
        arrived(j)[1].wait_recv()
    for h in range(heads):
        rows = [lse_out[group, h : h + 1, :]]
        parts = [share_out[h, group]]
        for j in range(1, members):
            member = lax.rem(group + j, members)
            remote(
                share_out.at[h, member],
                share_in.at[h, member],
                share_send.at[h, member],
                share_recv.at[h, member],
                peer,
            ).wait_recv()
            rows.append(lse_in[member, h : h + 1, :])
            parts.append(share_in[h, member])
        top = functools.reduce(jnp.maximum, rows)
        factors = [jnp.exp2(row - top) for row in rows]
        inverse = 1.0 / functools.reduce(jnp.add, factors)
        summed = functools.reduce(
            jnp.add,
            [
                part.astype(jnp.float32) * (factor * inverse)
                for part, factor in zip(parts, factors)
            ],
        )
        out_ref[:, h * dim : (h + 1) * dim] = summed.T.astype(out_ref.dtype)

    for h in range(heads):
        for j in range(1, frames):
            past_copy(h, j).wait_send()
            late_forward(h, j - 1).wait_send()
        for j in range(2):
            early_forward(h, j).wait_send()
        for j in range(1, members):
            query_copy(h, j).wait_send()
            share_copy(h, lax.rem(group + j, members)).wait_send()
    for j in range(1, members):
        lse_copy(j).wait_send()


def body(qkv_now, past_cache, frame_rank, frame_depth, tile_lists):
    toks, heads, width = qkv_now.shape
    dim = width // 3
    frames = lax.axis_size("frame")
    members = lax.axis_size("space") // 2
    past = jnp.transpose(past_cache[0], (1, 0, 2))
    qkv = jnp.transpose(qkv_now, (1, 0, 2))
    lse_rows = -(-heads // 8) * 8
    bias_count = -(-2 * (frames + 1) // 8) * 8
    half = members // 2
    dma = pltpu.SemaphoreType.DMA
    smem = pl.BlockSpec(memory_space=pltpu.SMEM)
    return pl.pallas_call(
        functools.partial(attend, frames, members, heads),
        out_shape=jax.ShapeDtypeStruct((toks, heads * dim), jnp.bfloat16),
        in_specs=[smem, smem, smem] + [pl.BlockSpec(memory_space=pl.ANY)] * 2,
        out_specs=pl.BlockSpec(memory_space=pltpu.VMEM),
        scratch_shapes=[
            pltpu.VMEM((2, heads, 2, toks, 2 * dim), jnp.bfloat16),
            pltpu.VMEM((2, heads, frames - 1, toks, 2 * dim), jnp.bfloat16),
            pltpu.VMEM((heads, members, toks, dim), jnp.bfloat16),
            pltpu.VMEM((dim, 4 * toks), jnp.bfloat16),
            pltpu.VMEM((dim, 2 * (frames - 1) * toks), jnp.bfloat16),
            pltpu.VMEM((half, bias_count, 2 * toks), jnp.float32),
            pltpu.VMEM((heads, half, dim, 2 * toks), jnp.float32),
            pltpu.VMEM((heads, half, 8, 2 * toks), jnp.float32),
            pltpu.VMEM((heads, members, dim, toks), jnp.bfloat16),
            pltpu.VMEM((heads, members, dim, toks), jnp.bfloat16),
            pltpu.VMEM((members, lse_rows, toks), jnp.float32),
            pltpu.VMEM((members, lse_rows, toks), jnp.float32),
            dma((heads, 3)),
            dma((heads, frames)),
            dma((heads, frames)),
            dma((heads, frames + 1)),
            dma((heads, frames + 1)),
            dma((heads, members)),
            dma((heads, members)),
            dma((heads, members)),
            dma((heads, members)),
            dma((members,)),
            dma((members,)),
        ],
        compiler_params=pltpu.CompilerParams(
            collective_id=0, has_side_effects=True, vmem_limit_bytes=48 * 1024 * 1024
        ),
    )(frame_rank, frame_depth, tile_lists, past, qkv)


def solution(mesh):
    in_specs = (P("space", "frame", None), P("frame", "space", None, None), P(), P(), P())
    out_specs = P("space", "frame")
    return jax.shard_map(body, mesh=mesh, in_specs=in_specs, out_specs=out_specs, check_vma=False)
```
